1024 devices in a mesh: ax: 256 (over z_lo, y, x, core), az: 4 (over z_hi).
Axes of the slice: x: 4, y: 4, z: 32 (z_hi: 4, z_lo: 8; z = z_hi * 8 + z_lo), core: 2. Of those that a mesh axis runs over, the one named last changes fastest.
Arguments:
- conserved: float32 [1024, 5, 32, 512], P('ax', None, None, 'az'), may hold values from -1.1 to 6.2, as said below
- cycle_modes: int32 [32], replicated, may hold values from 1 to 64, as said below
- filtered_cycles: int32 [1024], P('ax'), may hold values from 1 to 32, as said below
Outputs:
- stepped: float32 [1024, 5, 32, 512], P('ax', None, None, 'az')
The draws below stay inside these ranges and needn't reach their ends.
Inputs may be any that keep to these rules, and one draw needn't show every extreme that they name: `conserved`: density is at least 0.3 and pressure at least 0.02 in every cell. `cycle_modes`: 64 and 1 both occur. `filtered_cycles`: 32 and 1 both occur.
All inputs are finite; a program needn't handle non-finite values.
Results may differ from the reference program's by a relative error of at most 0.0003.
Values sent between devices are 32-bit elements; how exact they have to be, the bound alone decides.
A program may use at most 32 MiB of HBM per device.

```python
import math
import jax
import jax.numpy as jnp
from jax import lax

NR = 32
NT = 512
NRF = 32
MODE_MOST = 64
NX = 1024


def draw_conserved(key, part):
    keys = jax.random.split(key, 5)
    grid_shape = (NX, NR, NT)
    density = jnp.exp(jax.random.uniform(keys[0], grid_shape, jnp.float32, math.log(0.5), math.log(2.0)))
    pressure = jnp.exp(jax.random.uniform(keys[4], grid_shape, jnp.float32, math.log(0.03), math.log(0.1)))
    axial_vel = 1.5 + 0.2 * jnp.clip(jax.random.normal(keys[1], grid_shape, jnp.float32), -2.5, 2.5)
    radial_vel = 0.14 * jnp.clip(jax.random.normal(keys[2], grid_shape, jnp.float32), -2.5, 2.5)
    swirl_vel = 0.14 * jnp.clip(jax.random.normal(keys[3], grid_shape, jnp.float32), -2.5, 2.5)
    energy = pressure / 0.4 + 0.5 * density * (axial_vel * axial_vel + radial_vel * radial_vel + swirl_vel * swirl_vel)
    fields = jnp.stack([density, density * axial_vel, density * radial_vel, density * swirl_vel, energy], axis=1)
    return fields.astype(jnp.float32)


def draw_cycle_modes(key, part):
    keys = jax.random.split(jax.random.fold_in(key, 11), 3)
    base_modes = jax.random.randint(keys[0], (NRF,), 1, MODE_MOST + 1)
    top_cycle = jax.random.randint(keys[1], (), 0, NRF)
    low_cycle = (top_cycle + 1 + jax.random.randint(keys[2], (), 0, NRF - 1)) % NRF
    cycle_ids = jnp.arange(NRF, dtype=jnp.int32)
    modes = jnp.where(cycle_ids == top_cycle, MODE_MOST, jnp.where(cycle_ids == low_cycle, 1, base_modes))
    return modes.astype(jnp.int32)


def draw_filtered_cycles(key, part):
    keys = jax.random.split(jax.random.fold_in(key, 23), 3)
    base_counts = jax.random.randint(keys[0], (NX,), 1, NRF + 1)
    top_station = jax.random.randint(keys[1], (), 0, NX)
    low_station = (top_station + 1 + jax.random.randint(keys[2], (), 0, NX - 1)) % NX
    station_ids = jnp.arange(NX, dtype=jnp.int32)
    counts = jnp.where(station_ids == top_station, NRF, jnp.where(station_ids == low_station, 1, base_counts))
    return counts.astype(jnp.int32)


def setup_inputs(seed: int = 0) -> dict:
    arg_keys = jax.random.split(jax.random.key(seed), 4)
    return {
        "conserved": draw_conserved(jax.random.fold_in(arg_keys[3], 71), 0),
        "cycle_modes": draw_cycle_modes(jax.random.fold_in(arg_keys[3], 71), 0),
        "filtered_cycles": draw_filtered_cycles(jax.random.fold_in(arg_keys[3], 71), 0),
    }


STENCIL = (0.8, -0.2, 4.0 / 105.0, -1.0 / 280.0)
GAS_FACTOR = 0.4
TIME_STEP = 0.1


def velocities(fields):
    density = fields[:, 0]
    axial_vel = fields[:, 1] / density
    radial_vel = fields[:, 2] / density
    swirl_vel = fields[:, 3] / density
    kinetic = fields[:, 1] * axial_vel + fields[:, 2] * radial_vel + fields[:, 3] * swirl_vel
    pressure = GAS_FACTOR * (fields[:, 4] - 0.5 * kinetic)
    return axial_vel, radial_vel, swirl_vel, pressure


def axial_flux(fields):
    axial_vel, radial_vel, swirl_vel, pressure = velocities(fields)
    return jnp.stack([fields[:, 1], fields[:, 1] * axial_vel + pressure, fields[:, 2] * axial_vel,
                      fields[:, 3] * axial_vel, axial_vel * (fields[:, 4] + pressure)], axis=1)


def radial_flux(fields):
    axial_vel, radial_vel, swirl_vel, pressure = velocities(fields)
    return jnp.stack([fields[:, 2], fields[:, 1] * radial_vel, fields[:, 2] * radial_vel + pressure,
                      fields[:, 3] * radial_vel, radial_vel * (fields[:, 4] + pressure)], axis=1)


def swirl_flux(fields):
    axial_vel, radial_vel, swirl_vel, pressure = velocities(fields)
    return jnp.stack([fields[:, 3], fields[:, 1] * swirl_vel, fields[:, 2] * swirl_vel,
                      fields[:, 3] * swirl_vel + pressure, swirl_vel * (fields[:, 4] + pressure)], axis=1)


def central_difference(values, along, extent):
    result = None
    for offset, weight in zip((1, 2, 3, 4), STENCIL):
        forward_part = lax.slice_in_dim(values, 4 + offset, 4 + offset + extent, axis=along)
        backward_part = lax.slice_in_dim(values, 4 - offset, 4 - offset + extent, axis=along)
        contribution = weight * (forward_part - backward_part)
        result = contribution if result is None else result + contribution
    return result


def section_update(axial_padded, theta_padded, opposite, fields):
    stations = fields.shape[0]
    radial = fields.shape[2]
    width = fields.shape[3]
    axial_term = central_difference(axial_flux(axial_padded), 0, stations)
    flips = jnp.array([1.0, 1.0, -1.0, -1.0, 1.0], jnp.float32).reshape(1, 5, 1, 1)
    mirrored = opposite[:, :, ::-1, :] * flips
    outer_rows = jnp.broadcast_to(fields[:, :, -1:, :], (stations, 5, 4, width))
    radial_padded = jnp.concatenate([mirrored, fields, outer_rows], axis=2)
    signed_radius = (jnp.arange(radial + 8, dtype=jnp.float32) - 3.5).reshape(1, 1, -1, 1)
    radial_term = central_difference(radial_flux(radial_padded) * signed_radius, 2, radial)
    swirl_term = central_difference(swirl_flux(theta_padded), 3, width) * (NT / (2.0 * math.pi))
    axial_vel, radial_vel, swirl_vel, pressure = velocities(fields)
    nothing = jnp.zeros_like(pressure)
    source = jnp.stack([nothing, nothing, fields[:, 3] * swirl_vel + pressure,
                        -fields[:, 2] * swirl_vel, nothing], axis=1)
    radius = (jnp.arange(radial, dtype=jnp.float32) + 0.5).reshape(1, 1, -1, 1)
    tendency = -axial_term - (radial_term + swirl_term - source) / radius
    return fields + TIME_STEP * tendency


def fourier_basis(columns):
    harmonic = jnp.arange(2 * MODE_MOST, dtype=jnp.int32) % MODE_MOST
    product = (columns.astype(jnp.int32)[:, None] * harmonic[None, :]) % NT
    angle = product.astype(jnp.float32) * (2.0 * math.pi / NT)
    cosine_side = (jnp.arange(2 * MODE_MOST, dtype=jnp.int32) < MODE_MOST)[None, :]
    return jnp.where(cosine_side, jnp.cos(angle), jnp.sin(angle)).astype(jnp.float32)


def mode_weights(cycle_modes):
    harmonic = jnp.arange(2 * MODE_MOST, dtype=jnp.int32) % MODE_MOST
    base_weight = jnp.where(harmonic == 0, 1.0 / NT, 2.0 / NT).astype(jnp.float32)
    keep = harmonic[None, :] < cycle_modes[:, None]
    return jnp.where(keep, base_weight[None, :], 0.0).astype(jnp.float32)


def reference(conserved, cycle_modes, filtered_cycles):
    stations = conserved.shape[0]
    block = 8 if stations % 8 == 0 else 1
    basis = fourier_basis(jnp.arange(NT, dtype=jnp.int32))
    kept_weights = mode_weights(cycle_modes)
    cycle_ids = jnp.arange(NRF, dtype=jnp.int32)

    def one_block(first_row):
        rows = jnp.clip(first_row - 4 + jnp.arange(block + 8, dtype=jnp.int32), 0, stations - 1)
        axial_padded = jnp.take(conserved, rows, axis=0)
        center = lax.dynamic_slice_in_dim(conserved, first_row, block, 0)
        theta_padded = jnp.concatenate([center[..., -4:], center, center[..., :4]], axis=3)
        opposite = jnp.roll(center[:, :, :4, :], NT // 2, axis=3)
        section = section_update(axial_padded, theta_padded, opposite, center)
        inner_cycles = section[:, :, :NRF, :]
        coefficients = jnp.einsum("afrt,tc->afrc", inner_cycles, basis, precision=lax.Precision.HIGHEST)
        smoothed = jnp.einsum("afrc,tc->afrt", coefficients * kept_weights[None, None], basis,
                              precision=lax.Precision.HIGHEST)
        counts = lax.dynamic_slice_in_dim(filtered_cycles, first_row, block, 0)
        chosen = jnp.where(cycle_ids[None, None, :, None] < counts[:, None, None, None], smoothed, inner_cycles)
        return jnp.concatenate([chosen, section[:, :, NRF:, :]], axis=2)

    firsts = jnp.arange(0, stations, block, dtype=jnp.int32)
    blocks = lax.map(one_block, firsts)
    return blocks.reshape(conserved.shape)
```

```python
import functools
import math

import jax
import jax.numpy as jnp
import numpy as np
from jax import lax
from jax.experimental import pallas as pl
from jax.experimental.pallas import tpu as pltpu
from jax.sharding import PartitionSpec as P

NT = 512
NRF = 32
MODE_MOST = 64
STENCIL = (0.8, -0.2, 4.0 / 105.0, -1.0 / 280.0)
GAS_FACTOR = 0.4
TIME_STEP = 0.1

SECTORS = 4
WIDTH = NT // SECTORS
STATIONS = 4
FIELDS = 5
ROWS = 32
LINES = STATIONS * ROWS
NEAR = 12
FAR = 6
MESH = pl.DeviceIdType.MESH
EXACT = lax.Precision.HIGHEST
MIRROR_SIGNS = (1.0, 1.0, -1.0, -1.0, 1.0)


def kernel_factors(distance, rank):
    cells = np.arange(WIDTH)
    gap = WIDTH * distance + cells[:, None] - cells[None, :]
    left, values, right = np.linalg.svd(1.0 / np.sin(np.pi * gap / NT))
    root = np.sqrt(values[:rank])
    return (left[:, :rank] * root).T, right[:rank] * root[:, None]


def build_tables():
    parts = {}
    radius = np.arange(ROWS) + 0.5
    ring = np.zeros((ROWS, ROWS))
    mirror = np.zeros((4, ROWS))
    for row in range(ROWS):
        for k, weight in enumerate(STENCIL, 1):
            ring[row, min(row + k, ROWS - 1)] -= TIME_STEP * weight * (row + k + 0.5) / radius[row]
            below = row - k
            if below >= 0:
                ring[row, below] += TIME_STEP * weight * (below + 0.5) / radius[row]
            else:
                mirror[row, -1 - below] += TIME_STEP * weight * (-below - 0.5) / radius[row]
    parts["radial"] = np.kron(np.eye(STATIONS), ring)
    parts["mirror"] = np.kron(np.eye(STATIONS), mirror)
    swirl = np.zeros((WIDTH, WIDTH))
    edge = np.zeros((8, WIDTH))
    place = np.zeros((8, WIDTH))
    for cell in range(-4, WIDTH + 4):
        for k, weight in enumerate(STENCIL, 1):
            for source, value in ((cell + k, -weight), (cell - k, weight)):
                if 0 <= source < WIDTH:
                    if cell < 0:
                        edge[cell + 4, source] += value
                    elif cell >= WIDTH:
                        edge[cell - WIDTH + 4, source] += value
                    else:
                        swirl[source, cell] += value
    for cell in range(4):
        place[cell, WIDTH - 4 + cell] = 1.0
        place[4 + cell, cell] = 1.0
    parts["swirl"] = swirl
    parts["edge"] = edge
    parts["place"] = place
    angle = 2.0 * np.pi / NT * np.arange(WIDTH)[:, None] * np.arange(MODE_MOST)[None, :]
    parts["basis"] = np.concatenate([np.cos(angle), np.sin(angle)], axis=1)
    source_a = np.zeros((64, WIDTH))
    source_b = np.zeros((64, WIDTH))
    target_a = np.zeros((64, WIDTH))
    target_b = np.zeros((64, WIDTH))
    first = 0
    for distance, rank in ((1, NEAR), (-1, NEAR), (2, FAR)):
        target, source = kernel_factors(distance, rank)
        source_a[first : first + rank] = source
        source_b[first + rank : first + 2 * rank] = source
        target_a[first : first + rank] = target / NT
        target_b[first + rank : first + 2 * rank] = -target / NT
        first += 2 * rank
    parts["source_a"] = source_a
    parts["source_b"] = source_b
    parts["target_a"] = target_a
    parts["target_b"] = target_b
    spans, blocks, start = {}, [], 0
    for name, block in parts.items():
        spans[name] = (start, start + block.shape[0])
        start += block.shape[0]
        blocks.append(block)
    return np.concatenate(blocks, axis=0).astype(np.float32), spans


TABLES, SPANS = build_tables()
NEAR_ROWS = 2 * NEAR
FAR_ROWS = 2 * FAR
MESSAGE_ROWS = 2 * NEAR_ROWS + FAR_ROWS


def matmul(left, right, dims=((1,), (0,))):
    return lax.dot_general(left, right, (dims, ((), ())), precision=EXACT, preferred_element_type=jnp.float32)


def sector_waves(modes, sector):
    cell = lax.broadcasted_iota(jnp.int32, modes.shape, 1) + sector * WIDTH
    turn = ((2 * modes - 1) * cell) & (2 * NT - 1)
    angle = turn.astype(jnp.float32) * (math.pi / NT)
    return jnp.cos(angle), jnp.sin(angle)


def body(
    conserved, tables, modes, counts, out,
    cells, table, flux_f, flux_g, flux_h,
    axial_out, axial_in, edge_out, edge_in, mirror_out, mirror_in, mirror_mod,
    extra_out, extra_in, extra_own, section, modulated, message_out, message_in, compact,
    load_sem, send_sem, recv_sem,
):
    ax = lax.axis_index("ax")
    az = lax.axis_index("az")
    ax_count = lax.axis_size("ax")
    right = lax.rem(az + 1, SECTORS)
    left = lax.rem(az + SECTORS - 1, SECTORS)
    across = lax.rem(az + 2, SECTORS)
    has_low = ax > 0
    has_high = ax < ax_count - 1

    barrier = pltpu.get_barrier_semaphore()
    for sector in (right, left, across):
        pl.semaphore_signal(barrier, inc=1, device_id=(ax, sector), device_id_type=MESH)

    @pl.when(has_low)
    def _():
        pl.semaphore_signal(barrier, inc=1, device_id=(ax - 1, az), device_id_type=MESH)

    @pl.when(has_high)
    def _():
        pl.semaphore_signal(barrier, inc=1, device_id=(ax + 1, az), device_id_type=MESH)

    load_cells = pltpu.make_async_copy(conserved, cells, load_sem.at[0])
    load_table = pltpu.make_async_copy(tables, table, load_sem.at[1])
    load_cells.start()
    load_table.start()

    def tab(name):
        low, high = SPANS[name]
        return table[low:high]

    row = lax.broadcasted_iota(jnp.int32, (8, WIDTH), 0)
    lane = lax.broadcasted_iota(jnp.int32, (8, WIDTH), 1)
    mode_tiles = []
    for tile in range(ROWS // 8):
        value = jnp.zeros((8, WIDTH), jnp.int32)
        for j in range(8):
            value = jnp.where(row == j, modes[tile * 8 + j], value)
        mode_tiles.append(value)
    ring_modes = jnp.concatenate(mode_tiles, axis=0)
    inner_modes = jnp.zeros((8, WIDTH), jnp.int32)
    for j in range(4):
        inner_modes = jnp.where((row & 3) == j, modes[j], inner_modes)
    wave_c, wave_s = sector_waves(ring_modes, az)
    inner_c, inner_s = sector_waves(inner_modes, az)
    across_c, across_s = sector_waves(inner_modes, across)
    harmonic = lane & (MODE_MOST - 1)
    base_weight = jnp.where(harmonic == 0, 1.0 / NT, 2.0 / NT).astype(jnp.float32)
    ring_harmonic = lax.broadcasted_iota(jnp.int32, (ROWS, WIDTH), 1) & (MODE_MOST - 1)
    ring_base = jnp.where(ring_harmonic == 0, 1.0 / NT, 2.0 / NT).astype(jnp.float32)
    ring_weight = jnp.where(ring_harmonic < ring_modes, ring_base, 0.0)
    inner_weight = jnp.where(harmonic < inner_modes, base_weight, 0.0)
    ring_row = lax.broadcasted_iota(jnp.int32, (ROWS, WIDTH), 0)
    per_radius = TIME_STEP / (ring_row.astype(jnp.float32) + 0.5)

    load_cells.wait()
    for x in range(STATIONS):
        s0, s1, s2, s3, s4 = (cells[x, c] for c in range(FIELDS))
        inverse = 1.0 / s0
        a = s1 * inverse
        b = s2 * inverse
        d = s3 * inverse
        p = GAS_FACTOR * (s4 - 0.5 * (s1 * a + s2 * b + s3 * d))
        e = s4 + p
        lines = pl.ds(x * ROWS, ROWS)
        flux_f[x, 0], flux_f[x, 1], flux_f[x, 2], flux_f[x, 3], flux_f[x, 4] = s1, s1 * a + p, s2 * a, s3 * a, a * e
        for c, value in enumerate((s2, s1 * b, s2 * b + p, s3 * b, b * e)):
            flux_g[c, lines] = value
        swirl_two = s2 * d
        swirl_three = s3 * d + p
        for c, value in enumerate((s3, s1 * d, swirl_two, swirl_three, d * e)):
            flux_h[c, lines] = value * (per_radius * (NT / (2.0 * math.pi)))
        for c, value in enumerate((s0, s1, s2 + per_radius * swirl_three, s3 - per_radius * swirl_two, s4)):
            section[c, lines] = value
    for c in range(FIELDS):
        for i in range(STATIONS):
            own = from_low = to_high = to_low = None
            for s in range(STATIONS):
                value = flux_f[s, c]
                if s != i:
                    weight = TIME_STEP * STENCIL[abs(s - i) - 1] * (-1.0 if s > i else 1.0)
                    own = weight * value if own is None else own + weight * value
                if s >= i:
                    term = TIME_STEP * STENCIL[3 + i - s] * value
                    to_high = term if to_high is None else to_high + term
                if s <= i:
                    term = -TIME_STEP * STENCIL[3 + s - i] * value
                    to_low = term if to_low is None else to_low + term
            section[c, pl.ds(i * ROWS, ROWS)] += own
            axial_out[1, i, c] = to_high
            axial_out[0, i, c] = to_low
            edge_weight = TIME_STEP * sum(STENCIL[i:])
            pl.when(jnp.logical_not(has_low))(
                functools.partial(store, axial_in, (0, i, c), edge_weight * flux_f[0, c])
            )
            edge_weight = -TIME_STEP * sum(STENCIL[3 - i :])
            pl.when(jnp.logical_not(has_high))(
                functools.partial(store, axial_in, (1, i, c), edge_weight * flux_f[3, c])
            )

    load_table.wait()
    edges = matmul(tab("edge"), flux_h[...].reshape(FIELDS * LINES, WIDTH), ((1,), (1,)))
    edge_out[0] = edges[0:4]
    edge_out[1] = edges[4:8]

    def remote(source, target, slot, device):
        return pltpu.make_async_remote_copy(
            src_ref=source, dst_ref=target, send_sem=send_sem.at[slot], recv_sem=recv_sem.at[slot],
            device_id=device, device_id_type=MESH,
        )

    pl.semaphore_wait(barrier, 3 + has_low.astype(jnp.int32) + has_high.astype(jnp.int32))
    to_high = remote(axial_out.at[1], axial_in.at[0], 0, (ax + 1, az))
    to_low = remote(axial_out.at[0], axial_in.at[1], 1, (ax - 1, az))
    pl.when(has_high)(to_high.start)
    pl.when(has_low)(to_low.start)
    edge_left = remote(edge_out.at[0], edge_in.at[0], 2, (ax, left))
    edge_right = remote(edge_out.at[1], edge_in.at[1], 3, (ax, right))
    edge_left.start()
    edge_right.start()

    mirror_table = tab("mirror")
    for c in range(FIELDS):
        value = MIRROR_SIGNS[c] * matmul(mirror_table, flux_g[c])
        mirror_out[pl.ds(16 * c, 16)] = value
        for half in range(2):
            lines = pl.ds(16 * c + 8 * half, 8)
            mirror_mod[lines, 0:WIDTH] = value[8 * half : 8 * half + 8] * across_c
            mirror_mod[lines, WIDTH : 2 * WIDTH] = value[8 * half : 8 * half + 8] * across_s
    mirror_mod[80:128] = jnp.zeros((48, 2 * WIDTH), jnp.float32)
    mirror_copy = remote(mirror_out, mirror_in, 4, (ax, across))
    mirror_copy.start()
    sources = jnp.concatenate([tab("source_a"), tab("source_b")], axis=1)
    extra = matmul(sources, mirror_mod[...], ((1,), (1,)))
    extra_out[...] = extra[0 : 2 * NEAR_ROWS]
    extra_own[...] = extra[2 * NEAR_ROWS : 64]
    extra_left = remote(extra_out.at[0:NEAR_ROWS], extra_in.at[0:NEAR_ROWS], 5, (ax, left))
    extra_right = remote(
        extra_out.at[NEAR_ROWS : 2 * NEAR_ROWS], extra_in.at[NEAR_ROWS : 2 * NEAR_ROWS], 6, (ax, right)
    )
    extra_left.start()
    extra_right.start()

    radial_table = tab("radial")
    swirl_table = tab("swirl")
    for c in range(FIELDS):
        section[c] += matmul(radial_table, flux_g[c]) + matmul(flux_h[c], swirl_table)

    pl.when(has_high)(to_low_wait(remote(axial_out.at[1], axial_in.at[1], 1, (ax + 1, az))))
    pl.when(has_low)(to_low_wait(remote(axial_out.at[0], axial_in.at[0], 0, (ax - 1, az))))
    edge_left.wait_recv()
    edge_right.wait_recv()
    edges = jnp.concatenate([edge_in[0], edge_in[1]], axis=0)
    place = tab("place")
    for c in range(FIELDS):
        placed = matmul(edges[:, c * LINES : (c + 1) * LINES], place, ((0,), (0,)))
        for x in range(STATIONS):
            lines = pl.ds(x * ROWS, ROWS)
            value = section[c, lines] + placed[x * ROWS : (x + 1) * ROWS] + axial_in[0, x, c] + axial_in[1, x, c]
            section[c, lines] = value
            modulated[pl.ds(c * LINES + x * ROWS, ROWS), 0:WIDTH] = value * wave_c
            modulated[pl.ds(c * LINES + x * ROWS, ROWS), WIDTH : 2 * WIDTH] = value * wave_s
    messages = matmul(sources, modulated[...], ((1,), (1,)))
    message_out[...] = messages[0:MESSAGE_ROWS]
    spans = (
        (pl.ds(2 * NEAR_ROWS, FAR_ROWS), across),
        (pl.ds(0, NEAR_ROWS), right),
        (pl.ds(NEAR_ROWS, NEAR_ROWS), left),
    )
    message_copies = []
    for slot, (span, sector) in enumerate(spans, 7):
        copy = remote(message_out.at[span], message_in.at[span], slot, (ax, sector))
        copy.start()
        message_copies.append(copy)

    basis = tab("basis")
    for c in range(FIELDS):
        coefficients = matmul(section[c], basis)
        weighted = coefficients * jnp.concatenate([ring_weight] * STATIONS, axis=0)
        smoothed = matmul(weighted, basis, ((1,), (1,)))
        for x in range(STATIONS):
            modulated[pl.ds(c * LINES + x * ROWS, ROWS), 0:WIDTH] = smoothed[x * ROWS : (x + 1) * ROWS]

    part_row = lax.broadcasted_iota(jnp.int32, (64, 2 * WIDTH), 0)
    sign_left = jnp.where(az == 0, -1.0, 1.0)
    sign_right = jnp.where(az == SECTORS - 1, -1.0, 1.0)
    sign_across = jnp.where(az < 2, -1.0, 1.0)
    signs = jnp.where(part_row < NEAR_ROWS, sign_left, jnp.where(part_row < 2 * NEAR_ROWS, sign_right, sign_across))
    targets = jnp.concatenate([tab("target_a"), tab("target_b")], axis=1) * signs.astype(jnp.float32)

    extra_left.wait_recv()
    extra_right.wait_recv()
    extra = jnp.concatenate([extra_in[...], extra_own[...]], axis=0)
    extra_field = matmul(extra, targets, ((0,), (0,)))
    mirror_copy.wait_recv()
    mirrored = mirror_in[...]
    weighted = matmul(mirrored, basis) * jnp.concatenate([inner_weight] * 10, axis=0)
    compact_smooth = matmul(weighted, basis, ((1,), (1,)))
    for c in range(FIELDS):
        for half in range(2):
            lines = pl.ds(16 * c + 8 * half, 8)
            low = 16 * c + 8 * half
            smooth = (
                compact_smooth[low : low + 8]
                + inner_s * extra_field[low : low + 8, 0:WIDTH]
                + inner_c * extra_field[low : low + 8, WIDTH : 2 * WIDTH]
            )
            limit = jnp.where(row < 4, counts[2 * half], counts[2 * half + 1])
            compact[lines] = jnp.where((row & 3) < limit, smooth, mirror_in[lines])

    for copy in message_copies:
        copy.wait_recv()
    for c in range(FIELDS):
        field = matmul(message_in[:, c * LINES : (c + 1) * LINES], targets[0:MESSAGE_ROWS], ((0,), (0,)))
        for x in range(STATIONS):
            low = x * ROWS
            smooth = (
                modulated[pl.ds(c * LINES + low, ROWS), 0:WIDTH]
                + wave_s * field[low : low + ROWS, 0:WIDTH]
                + wave_c * field[low : low + ROWS, WIDTH : 2 * WIDTH]
            )
            out[x, c] = jnp.where(ring_row < counts[x], smooth, section[c, pl.ds(low, ROWS)])
            out[x, c, 0:4] += compact[pl.ds(16 * c + 4 * x, 4)]

    pl.when(has_high)(to_high.wait_send)
    pl.when(has_low)(to_low.wait_send)
    for copy in (edge_left, edge_right, mirror_copy, extra_left, extra_right, *message_copies):
        copy.wait_send()


def store(ref, index, value):
    ref[index] = value


def to_low_wait(copy):
    return copy.wait_recv


def per_device(conserved, cycle_modes, filtered_cycles):
    f32 = jnp.float32
    block = (STATIONS, FIELDS, ROWS, WIDTH)
    lines = FIELDS * LINES
    return pl.pallas_call(
        body,
        out_shape=jax.ShapeDtypeStruct(block, f32),
        in_specs=[
            pl.BlockSpec(memory_space=pl.ANY),
            pl.BlockSpec(memory_space=pl.ANY),
            pl.BlockSpec(memory_space=pltpu.SMEM),
            pl.BlockSpec(memory_space=pltpu.SMEM),
        ],
        out_specs=pl.BlockSpec(memory_space=pltpu.VMEM),
        scratch_shapes=[
            pltpu.VMEM(block, f32),
            pltpu.VMEM(TABLES.shape, f32),
            pltpu.VMEM(block, f32),
            pltpu.VMEM((FIELDS, LINES, WIDTH), f32),
            pltpu.VMEM((FIELDS, LINES, WIDTH), f32),
            pltpu.VMEM((2,) + block, f32),
            pltpu.VMEM((2,) + block, f32),
            pltpu.VMEM((2, 4, lines), f32),
            pltpu.VMEM((2, 4, lines), f32),
            pltpu.VMEM((80, WIDTH), f32),
            pltpu.VMEM((80, WIDTH), f32),
            pltpu.VMEM((128, 2 * WIDTH), f32),
            pltpu.VMEM((2 * NEAR_ROWS, WIDTH), f32),
            pltpu.VMEM((2 * NEAR_ROWS, WIDTH), f32),
            pltpu.VMEM((16, WIDTH), f32),
            pltpu.VMEM((FIELDS, LINES, WIDTH), f32),
            pltpu.VMEM((lines, 2 * WIDTH), f32),
            pltpu.VMEM((MESSAGE_ROWS, lines), f32),
            pltpu.VMEM((MESSAGE_ROWS, lines), f32),
            pltpu.VMEM((80, WIDTH), f32),
            pltpu.SemaphoreType.DMA((2,)),
            pltpu.SemaphoreType.DMA((10,)),
            pltpu.SemaphoreType.DMA((10,)),
        ],
        compiler_params=pltpu.CompilerParams(
            collective_id=0, has_side_effects=True, vmem_limit_bytes=32 * 1024 * 1024
        ),
    )(conserved, jnp.asarray(TABLES), cycle_modes, filtered_cycles)


def solution(mesh):
    placed = (P("ax", None, None, "az"), P(), P("ax"))
    return jax.shard_map(
        per_device, mesh=mesh, in_specs=placed, out_specs=P("ax", None, None, "az"), check_vma=False
    )
```

```python
import functools
import math

import jax
import jax.numpy as jnp
import numpy as np
from jax import lax
from jax.experimental import pallas as pl
from jax.experimental.pallas import tpu as pltpu
from jax.sharding import PartitionSpec as P

NT = 512
NRF = 32
MODE_MOST = 64
STENCIL = (0.8, -0.2, 4.0 / 105.0, -1.0 / 280.0)
GAS_FACTOR = 0.4
TIME_STEP = 0.1

SECTORS = 4
WIDTH = NT // SECTORS
STATIONS = 4
FIELDS = 5
ROWS = 32
LINES = STATIONS * ROWS
NEAR = 11
FAR = 5
MESH = pl.DeviceIdType.MESH
EXACT = lax.Precision.HIGHEST
MIRROR_SIGNS = (1.0, 1.0, -1.0, -1.0, 1.0)


def kernel_factors(distance, rank):
    cells = np.arange(WIDTH)
    gap = WIDTH * distance + cells[:, None] - cells[None, :]
    left, values, right = np.linalg.svd(1.0 / np.sin(np.pi * gap / NT))
    root = np.sqrt(values[:rank])
    return (left[:, :rank] * root).T, right[:rank] * root[:, None]


NEAR_ROWS = 2 * NEAR
FAR_ROWS = 2 * FAR
NEAR_PAD = 24
MESSAGE_ROWS = 64


def build_tables():
    parts = {}
    radius = np.arange(ROWS) + 0.5
    ring = np.zeros((ROWS, ROWS))
    mirror = np.zeros((4, ROWS))
    for row in range(ROWS):
        for k, weight in enumerate(STENCIL, 1):
            ring[row, min(row + k, ROWS - 1)] -= TIME_STEP * weight * (row + k + 0.5) / radius[row]
            below = row - k
            if below >= 0:
                ring[row, below] += TIME_STEP * weight * (below + 0.5) / radius[row]
            else:
                mirror[row, -1 - below] += TIME_STEP * weight * (-below - 0.5) / radius[row]
    parts["radial"] = np.kron(np.eye(STATIONS), ring)
    parts["mirror"] = np.kron(np.eye(STATIONS), mirror)
    swirl = np.zeros((WIDTH, WIDTH))
    edge = np.zeros((8, WIDTH))
    place = np.zeros((8, WIDTH))
    for cell in range(-4, WIDTH + 4):
        for k, weight in enumerate(STENCIL, 1):
            for source, value in ((cell + k, -weight), (cell - k, weight)):
                if 0 <= source < WIDTH:
                    if cell < 0:
                        edge[cell + 4, source] += value
                    elif cell >= WIDTH:
                        edge[cell - WIDTH + 4, source] += value
                    else:
                        swirl[source, cell] += value
    for cell in range(4):
        place[cell, WIDTH - 4 + cell] = 1.0
        place[4 + cell, cell] = 1.0
    parts["swirl"] = swirl
    parts["edge"] = edge
    parts["place"] = place
    angle = 2.0 * np.pi / NT * np.arange(WIDTH)[:, None] * np.arange(MODE_MOST)[None, :]
    parts["basis"] = np.concatenate([np.cos(angle), np.sin(angle)], axis=1)
    source_a = np.zeros((64, WIDTH))
    source_b = np.zeros((64, WIDTH))
    target_a = np.zeros((64, WIDTH))
    target_b = np.zeros((64, WIDTH))
    for distance, rank, first in ((1, NEAR, 0), (-1, NEAR, NEAR_PAD), (2, FAR, 2 * NEAR_PAD)):
        target, source = kernel_factors(distance, rank)
        source_a[first : first + rank] = source
        source_b[first + rank : first + 2 * rank] = source
        target_a[first : first + rank] = target / NT
        target_b[first + rank : first + 2 * rank] = -target / NT
    parts["source_a"] = source_a
    parts["source_b"] = source_b
    parts["target_a"] = target_a
    parts["target_b"] = target_b
    spans, blocks, start = {}, [], 0
    for name, block in parts.items():
        spans[name] = (start, start + block.shape[0])
        start += block.shape[0]
        blocks.append(block)
    return np.concatenate(blocks, axis=0).astype(np.float32), spans


TABLES, SPANS = build_tables()


def matmul(left, right, dims=((1,), (0,))):
    return lax.dot_general(left, right, (dims, ((), ())), precision=EXACT, preferred_element_type=jnp.float32)


def sector_waves(modes, sector):
    cell = lax.broadcasted_iota(jnp.int32, modes.shape, 1) + sector * WIDTH
    turn = ((2 * modes - 1) * cell) & (2 * NT - 1)
    angle = turn.astype(jnp.float32) * (math.pi / NT)
    return jnp.cos(angle), jnp.sin(angle)


def body(
    conserved, tables, modes, counts, out,
    cells, table, mode, count, flux_f, flux_g, flux_h,
    axial_out, axial_in, edge_out, edge_in, mirror_out, mirror_in, mirror_mod,
    extra_out, extra_in, extra_own, section, modulated, near_out, near_in, far_out, far_in, message, compact,
    load_sem, send_sem, recv_sem,
):
    ax = lax.axis_index("ax")
    az = lax.axis_index("az")
    ax_count = lax.axis_size("ax")
    right = lax.rem(az + 1, SECTORS)
    left = lax.rem(az + SECTORS - 1, SECTORS)
    across = lax.rem(az + 2, SECTORS)
    has_low = ax > 0
    has_high = ax < ax_count - 1

    barrier = pltpu.get_barrier_semaphore()
    for sector in (right, left):
        pl.semaphore_signal(barrier, inc=1, device_id=(ax, sector), device_id_type=MESH)

    @pl.when(has_low)
    def _():
        pl.semaphore_signal(barrier, inc=1, device_id=(ax - 1, az), device_id_type=MESH)

    @pl.when(has_high)
    def _():
        pl.semaphore_signal(barrier, inc=1, device_id=(ax + 1, az), device_id_type=MESH)

    load_cells = pltpu.make_async_copy(conserved, cells, load_sem.at[0])
    load_table = pltpu.make_async_copy(tables, table, load_sem.at[1])
    load_mode = pltpu.make_async_copy(modes, mode, load_sem.at[2])
    load_count = pltpu.make_async_copy(counts, count, load_sem.at[3])
    load_mode.start()
    load_count.start()
    load_cells.start()
    load_table.start()

    def tab(name):
        low, high = SPANS[name]
        return table[low:high]

    row = lax.broadcasted_iota(jnp.int32, (8, WIDTH), 0)
    lane = lax.broadcasted_iota(jnp.int32, (8, WIDTH), 1)
    lines_all = FIELDS * LINES
    for low, high in ((NEAR_ROWS, NEAR_PAD), (NEAR_PAD + NEAR_ROWS, 2 * NEAR_PAD), (2 * NEAR_PAD + FAR_ROWS, MESSAGE_ROWS)):
        message[low:high] = jnp.zeros((high - low, lines_all), jnp.float32)
    load_mode.wait()
    load_count.wait()
    mode_tiles = []
    for tile in range(ROWS // 8):
        value = jnp.zeros((8, WIDTH), jnp.int32)
        for j in range(8):
            value = jnp.where(row == j, mode[tile * 8 + j], value)
        mode_tiles.append(value)
    ring_modes = jnp.concatenate(mode_tiles, axis=0)
    inner_modes = jnp.zeros((8, WIDTH), jnp.int32)
    for j in range(4):
        inner_modes = jnp.where((row & 3) == j, mode[j], inner_modes)
    wave_c, wave_s = sector_waves(ring_modes, az)
    inner_c, inner_s = sector_waves(inner_modes, az)
    across_c, across_s = sector_waves(inner_modes, across)
    harmonic = lane & (MODE_MOST - 1)
    base_weight = jnp.where(harmonic == 0, 1.0 / NT, 2.0 / NT).astype(jnp.float32)
    ring_harmonic = lax.broadcasted_iota(jnp.int32, (ROWS, WIDTH), 1) & (MODE_MOST - 1)
    ring_base = jnp.where(ring_harmonic == 0, 1.0 / NT, 2.0 / NT).astype(jnp.float32)
    ring_weight = jnp.where(ring_harmonic < ring_modes, ring_base, 0.0)
    inner_weight = jnp.where(harmonic < inner_modes, base_weight, 0.0)
    ring_row = lax.broadcasted_iota(jnp.int32, (ROWS, WIDTH), 0)
    per_radius = TIME_STEP / (ring_row.astype(jnp.float32) + 0.5)

    load_cells.wait()
    for x in range(STATIONS):
        s0, s1, s2, s3, s4 = (cells[x, c] for c in range(FIELDS))
        inverse = 1.0 / s0
        a = s1 * inverse
        b = s2 * inverse
        d = s3 * inverse
        p = GAS_FACTOR * (s4 - 0.5 * (s1 * a + s2 * b + s3 * d))
        e = s4 + p
        lines = pl.ds(x * ROWS, ROWS)
        flux_f[x, 0], flux_f[x, 1], flux_f[x, 2], flux_f[x, 3], flux_f[x, 4] = s1, s1 * a + p, s2 * a, s3 * a, a * e
        for c, value in enumerate((s2, s1 * b, s2 * b + p, s3 * b, b * e)):
            flux_g[c, lines] = value
        swirl_two = s2 * d
        swirl_three = s3 * d + p
        for c, value in enumerate((s3, s1 * d, swirl_two, swirl_three, d * e)):
            flux_h[c, lines] = value * (per_radius * (NT / (2.0 * math.pi)))
        for c, value in enumerate((s0, s1, s2 + per_radius * swirl_three, s3 - per_radius * swirl_two, s4)):
            section[c, lines] = value
    for c in range(FIELDS):
        for i in range(STATIONS):
            own = from_low = to_high = to_low = None
            for s in range(STATIONS):
                value = flux_f[s, c]
                if s != i:
                    weight = TIME_STEP * STENCIL[abs(s - i) - 1] * (-1.0 if s > i else 1.0)
                    own = weight * value if own is None else own + weight * value
                if s >= i:
                    term = TIME_STEP * STENCIL[3 + i - s] * value
                    to_high = term if to_high is None else to_high + term
                if s <= i:
                    term = -TIME_STEP * STENCIL[3 + s - i] * value
                    to_low = term if to_low is None else to_low + term
            section[c, pl.ds(i * ROWS, ROWS)] += own
            axial_out[1, i, c] = to_high
            axial_out[0, i, c] = to_low
            edge_weight = TIME_STEP * sum(STENCIL[i:])
            pl.when(jnp.logical_not(has_low))(
                functools.partial(store, axial_in, (0, i, c), edge_weight * flux_f[0, c])
            )
            edge_weight = -TIME_STEP * sum(STENCIL[3 - i :])
            pl.when(jnp.logical_not(has_high))(
                functools.partial(store, axial_in, (1, i, c), edge_weight * flux_f[3, c])
            )

    load_table.wait()
    edges = matmul(tab("edge"), flux_h[...].reshape(FIELDS * LINES, WIDTH), ((1,), (1,)))
    edge_out[0] = edges[0:4]
    edge_out[1] = edges[4:8]

    def remote(source, target, slot, device):
        return pltpu.make_async_remote_copy(
            src_ref=source, dst_ref=target, send_sem=send_sem.at[slot], recv_sem=recv_sem.at[slot],
            device_id=device, device_id_type=MESH,
        )

    pl.semaphore_wait(barrier, 2 + has_low.astype(jnp.int32) + has_high.astype(jnp.int32))
    to_high = remote(axial_out.at[1], axial_in.at[0], 0, (ax + 1, az))
    to_low = remote(axial_out.at[0], axial_in.at[1], 1, (ax - 1, az))
    edge_left = remote(edge_out.at[0], edge_in.at[0], 2, (ax, left))
    edge_right = remote(edge_out.at[1], edge_in.at[1], 3, (ax, right))
    edge_left.start()
    edge_right.start()
    pl.when(has_high)(to_high.start)
    pl.when(has_low)(to_low.start)

    mirror_table = tab("mirror")
    for c in range(FIELDS):
        value = MIRROR_SIGNS[c] * matmul(mirror_table, flux_g[c])
        mirror_out[pl.ds(16 * c, 16)] = value
        for half in range(2):
            lines = pl.ds(16 * c + 8 * half, 8)
            mirror_mod[lines, 0:WIDTH] = value[8 * half : 8 * half + 8] * across_c
            mirror_mod[lines, WIDTH : 2 * WIDTH] = value[8 * half : 8 * half + 8] * across_s
    mirror_mod[80:128] = jnp.zeros((48, 2 * WIDTH), jnp.float32)
    mirror_copy = remote(mirror_out, mirror_in, 4, (ax, across))
    sources = jnp.concatenate([tab("source_a"), tab("source_b")], axis=1)
    extra = matmul(sources, mirror_mod[...], ((1,), (1,)))
    extra_out[...] = extra[0 : 2 * NEAR_PAD]
    extra_own[...] = extra[2 * NEAR_PAD : 64]
    extra_left = remote(extra_out.at[0:NEAR_PAD], extra_in.at[0:NEAR_PAD], 5, (ax, left))
    extra_right = remote(
        extra_out.at[NEAR_PAD : 2 * NEAR_PAD], extra_in.at[NEAR_PAD : 2 * NEAR_PAD], 6, (ax, right)
    )
    extra_left.start()
    extra_right.start()

    radial_table = tab("radial")
    swirl_table = tab("swirl")
    for c in range(FIELDS):
        section[c] += matmul(radial_table, flux_g[c]) + matmul(flux_h[c], swirl_table)

    pl.when(has_high)(to_low_wait(remote(axial_out.at[1], axial_in.at[1], 1, (ax + 1, az))))
    pl.when(has_low)(to_low_wait(remote(axial_out.at[0], axial_in.at[0], 0, (ax - 1, az))))
    for c in range(FIELDS):
        for x in range(STATIONS):
            section[c, pl.ds(x * ROWS, ROWS)] += axial_in[0, x, c] + axial_in[1, x, c]
    edge_left.wait_recv()
    edge_right.wait_recv()
    edges = jnp.concatenate([edge_in[0], edge_in[1]], axis=0)
    place = tab("place")
    for c in range(FIELDS):
        placed = matmul(edges[:, c * LINES : (c + 1) * LINES], place, ((0,), (0,)))
        for x in range(STATIONS):
            lines = pl.ds(x * ROWS, ROWS)
            value = section[c, lines] + placed[x * ROWS : (x + 1) * ROWS]
            section[c, lines] = value
            modulated[pl.ds(c * LINES + x * ROWS, ROWS), 0:WIDTH] = value * wave_c
            modulated[pl.ds(c * LINES + x * ROWS, ROWS), WIDTH : 2 * WIDTH] = value * wave_s
    messages = matmul(sources, modulated[...], ((1,), (1,)))
    far_out[...] = messages[2 * NEAR_PAD : 2 * NEAR_PAD + FAR_ROWS]
    far_copy = remote(far_out, far_in, 7, (ax, across))
    far_copy.start()
    mirror_copy.start()
    near_out[0] = messages[0:NEAR_ROWS]
    near_right = remote(near_out.at[0], near_in.at[0], 8, (ax, right))
    near_right.start()
    near_out[1] = messages[NEAR_PAD : NEAR_PAD + NEAR_ROWS]
    near_left = remote(near_out.at[1], near_in.at[1], 9, (ax, left))
    near_left.start()

    basis = tab("basis")
    for c in range(FIELDS):
        coefficients = matmul(section[c], basis)
        weighted = coefficients * jnp.concatenate([ring_weight] * STATIONS, axis=0)
        smoothed = matmul(weighted, basis, ((1,), (1,)))
        for x in range(STATIONS):
            modulated[pl.ds(c * LINES + x * ROWS, ROWS), 0:WIDTH] = smoothed[x * ROWS : (x + 1) * ROWS]

    part_row = lax.broadcasted_iota(jnp.int32, (64, 2 * WIDTH), 0)
    sign_left = jnp.where(az == 0, -1.0, 1.0)
    sign_right = jnp.where(az == SECTORS - 1, -1.0, 1.0)
    sign_across = jnp.where(az < 2, -1.0, 1.0)
    signs = jnp.where(part_row < NEAR_PAD, sign_left, jnp.where(part_row < 2 * NEAR_PAD, sign_right, sign_across))
    targets = jnp.concatenate([tab("target_a"), tab("target_b")], axis=1) * signs.astype(jnp.float32)

    extra_left.wait_recv()
    extra_right.wait_recv()
    extra = jnp.concatenate([extra_in[...], extra_own[...]], axis=0)
    extra_field = matmul(extra, targets, ((0,), (0,)))
    mirror_copy.wait_recv()
    mirrored = mirror_in[...]
    weighted = matmul(mirrored, basis) * jnp.concatenate([inner_weight] * 10, axis=0)
    compact_smooth = matmul(weighted, basis, ((1,), (1,)))
    for c in range(FIELDS):
        for half in range(2):
            lines = pl.ds(16 * c + 8 * half, 8)
            low = 16 * c + 8 * half
            smooth = (
                compact_smooth[low : low + 8]
                + inner_s * extra_field[low : low + 8, 0:WIDTH]
                + inner_c * extra_field[low : low + 8, WIDTH : 2 * WIDTH]
            )
            limit = jnp.where(row < 4, count[2 * half], count[2 * half + 1])
            compact[lines] = jnp.where((row & 3) < limit, smooth, mirror_in[lines])

    far_copy.wait_recv()
    message[2 * NEAR_PAD : 2 * NEAR_PAD + FAR_ROWS] = far_in[...]
    near_right.wait_recv()
    message[0:NEAR_ROWS] = near_in[0]
    near_left.wait_recv()
    message[NEAR_PAD : NEAR_PAD + NEAR_ROWS] = near_in[1]
    for c in range(FIELDS):
        field = matmul(message[:, c * LINES : (c + 1) * LINES], targets, ((0,), (0,)))
        for x in range(STATIONS):
            low = x * ROWS
            smooth = (
                modulated[pl.ds(c * LINES + low, ROWS), 0:WIDTH]
                + wave_s * field[low : low + ROWS, 0:WIDTH]
                + wave_c * field[low : low + ROWS, WIDTH : 2 * WIDTH]
            )
            out[x, c] = jnp.where(ring_row < count[x], smooth, section[c, pl.ds(low, ROWS)])
            out[x, c, 0:4] += compact[pl.ds(16 * c + 4 * x, 4)]

    pl.when(has_high)(to_high.wait_send)
    pl.when(has_low)(to_low.wait_send)
    for copy in (edge_left, edge_right, mirror_copy, extra_left, extra_right, far_copy, near_right, near_left):
        copy.wait_send()


def store(ref, index, value):
    ref[index] = value


def to_low_wait(copy):
    return copy.wait_recv


def per_device(conserved, cycle_modes, filtered_cycles):
    f32 = jnp.float32
    block = (STATIONS, FIELDS, ROWS, WIDTH)
    lines = FIELDS * LINES
    return pl.pallas_call(
        body,
        out_shape=jax.ShapeDtypeStruct(block, f32),
        in_specs=[
            pl.BlockSpec(memory_space=pltpu.HBM),
            pl.BlockSpec(memory_space=pltpu.HBM),
            pl.BlockSpec(memory_space=pltpu.HBM),
            pl.BlockSpec(memory_space=pltpu.HBM),
        ],
        out_specs=pl.BlockSpec(memory_space=pltpu.VMEM),
        scratch_shapes=[
            pltpu.VMEM(block, f32),
            pltpu.VMEM(TABLES.shape, f32),
            pltpu.SMEM((ROWS,), jnp.int32),
            pltpu.SMEM((STATIONS,), jnp.int32),
            pltpu.VMEM(block, f32),
            pltpu.VMEM((FIELDS, LINES, WIDTH), f32),
            pltpu.VMEM((FIELDS, LINES, WIDTH), f32),
            pltpu.VMEM((2,) + block, f32),
            pltpu.VMEM((2,) + block, f32),
            pltpu.VMEM((2, 4, lines), f32),
            pltpu.VMEM((2, 4, lines), f32),
            pltpu.VMEM((80, WIDTH), f32),
            pltpu.VMEM((80, WIDTH), f32),
            pltpu.VMEM((128, 2 * WIDTH), f32),
            pltpu.VMEM((2 * NEAR_PAD, WIDTH), f32),
            pltpu.VMEM((2 * NEAR_PAD, WIDTH), f32),
            pltpu.VMEM((16, WIDTH), f32),
            pltpu.VMEM((FIELDS, LINES, WIDTH), f32),
            pltpu.VMEM((lines, 2 * WIDTH), f32),
            pltpu.VMEM((2, NEAR_ROWS, lines), f32),
            pltpu.VMEM((2, NEAR_ROWS, lines), f32),
            pltpu.VMEM((FAR_ROWS, lines), f32),
            pltpu.VMEM((FAR_ROWS, lines), f32),
            pltpu.VMEM((MESSAGE_ROWS, lines), f32),
            pltpu.VMEM((80, WIDTH), f32),
            pltpu.SemaphoreType.DMA((4,)),
            pltpu.SemaphoreType.DMA((10,)),
            pltpu.SemaphoreType.DMA((10,)),
        ],
        compiler_params=pltpu.CompilerParams(
            collective_id=0, has_side_effects=True, vmem_limit_bytes=60 * 1024 * 1024
        ),
    )(conserved, jnp.asarray(TABLES), cycle_modes, filtered_cycles)


def solution(mesh):
    placed = (P("ax", None, None, "az"), P(), P("ax"))
    return jax.shard_map(
        per_device, mesh=mesh, in_specs=placed, out_specs=P("ax", None, None, "az"), check_vma=False
    )
```

```python
import functools
import math

import jax
import jax.numpy as jnp
import numpy as np
from jax import lax
from jax.experimental import pallas as pl
from jax.experimental.pallas import tpu as pltpu
from jax.sharding import PartitionSpec as P

NT = 512
NRF = 32
MODE_MOST = 64
STENCIL = (0.8, -0.2, 4.0 / 105.0, -1.0 / 280.0)
GAS_FACTOR = 0.4
TIME_STEP = 0.1

SECTORS = 4
WIDTH = NT // SECTORS
STATIONS = 4
FIELDS = 5
ROWS = 32
LINES = STATIONS * ROWS
NEAR = 10
FAR = 5
MESH = pl.DeviceIdType.MESH
EXACT = lax.Precision.HIGHEST
MIRROR_SIGNS = (1.0, 1.0, -1.0, -1.0, 1.0)


def kernel_factors(distance, rank, sources):
    gap = WIDTH * distance + np.arange(WIDTH)[:, None] - sources[None, :]
    left, values, right = np.linalg.svd(1.0 / np.sin(np.pi * gap / NT))
    root = np.sqrt(values[:rank])
    return (left[:, :rank] * root).T, right[:rank] * root[:, None]


NEAR_ROWS = 2 * NEAR
FAR_ROWS = 2 * FAR
NEAR_PAD = 24
MESSAGE_ROWS = 64


def build_tables():
    parts = {}
    radius = np.arange(ROWS) + 0.5
    ring = np.zeros((ROWS, ROWS))
    mirror = np.zeros((4, ROWS))
    for row in range(ROWS):
        for k, weight in enumerate(STENCIL, 1):
            ring[row, min(row + k, ROWS - 1)] -= TIME_STEP * weight * (row + k + 0.5) / radius[row]
            below = row - k
            if below >= 0:
                ring[row, below] += TIME_STEP * weight * (below + 0.5) / radius[row]
            else:
                mirror[row, -1 - below] += TIME_STEP * weight * (-below - 0.5) / radius[row]
    parts["radial"] = np.kron(np.eye(STATIONS), ring)
    parts["mirror"] = np.kron(np.eye(STATIONS), mirror)
    swirl = np.zeros((WIDTH, WIDTH))
    edge = np.zeros((8, WIDTH))
    place = np.zeros((8, WIDTH))
    for cell in range(-4, WIDTH + 4):
        for k, weight in enumerate(STENCIL, 1):
            for source, value in ((cell + k, -weight), (cell - k, weight)):
                if 0 <= source < WIDTH:
                    if cell < 0:
                        edge[cell + 4, source] += value
                    elif cell >= WIDTH:
                        edge[cell - WIDTH + 4, source] += value
                    else:
                        swirl[source, cell] += value
    for cell in range(4):
        place[cell, WIDTH - 4 + cell] = 1.0
        place[4 + cell, cell] = 1.0
    parts["swirl"] = swirl
    parts["edge"] = edge
    parts["place"] = place
    angle = 2.0 * np.pi / NT * np.arange(WIDTH)[:, None] * np.arange(MODE_MOST)[None, :]
    parts["basis"] = np.concatenate([np.cos(angle), np.sin(angle)], axis=1)
    source_a = np.zeros((64, WIDTH))
    source_b = np.zeros((64, WIDTH))
    target_a = np.zeros((64, WIDTH))
    target_b = np.zeros((64, WIDTH))
    source_edge = np.zeros((2 * MESSAGE_ROWS, WIDTH))
    for distance, rank, first, low, high in (
        (1, NEAR, 0, -4, WIDTH),
        (-1, NEAR, NEAR_PAD, 0, WIDTH + 4),
        (2, FAR, 2 * NEAR_PAD, -4, WIDTH + 4),
    ):
        target, source = kernel_factors(distance, rank, np.arange(low, high))
        own = source[:, -low : WIDTH - low]
        for wave, (into, out_of, half) in enumerate(((source_a, target_a, 1.0 / NT), (source_b, target_b, -1.0 / NT))):
            rows = slice(first + wave * rank, first + (wave + 1) * rank)
            back = slice(MESSAGE_ROWS + rows.start, MESSAGE_ROWS + rows.stop)
            into[rows] = own
            out_of[rows] = half * target
            if low < 0:
                source_edge[rows, 8 * wave : 8 * wave + 4] = source[:, 0:4]
            if high > WIDTH:
                source_edge[rows, 8 * wave + 4 : 8 * wave + 8] = source[:, -4:]
            if distance == 1:
                source_edge[back, 8 * wave : 8 * wave + 4] = own[:, -4:]
            if distance == -1:
                source_edge[back, 8 * wave + 4 : 8 * wave + 8] = own[:, 0:4]
    parts["source_a"] = source_a
    parts["source_b"] = source_b
    parts["source_edge"] = source_edge
    parts["target_a"] = target_a
    parts["target_b"] = target_b
    spans, blocks, start = {}, [], 0
    for name, block in parts.items():
        spans[name] = (start, start + block.shape[0])
        start += block.shape[0]
        blocks.append(block)
    return np.concatenate(blocks, axis=0).astype(np.float32), spans


TABLES, SPANS = build_tables()


def matmul(left, right, dims=((1,), (0,))):
    return lax.dot_general(left, right, (dims, ((), ())), precision=EXACT, preferred_element_type=jnp.float32)


def sector_waves(modes, sector):
    return waves(modes, lax.broadcasted_iota(jnp.int32, modes.shape, 1) + sector * WIDTH)


def waves(modes, cell):
    turn = ((2 * modes - 1) * cell) & (2 * NT - 1)
    angle = turn.astype(jnp.float32) * (math.pi / NT)
    return jnp.cos(angle), jnp.sin(angle)


def body(
    conserved, tables, modes, counts, out,
    cells, table, mode, count, flux_f, flux_g, flux_h,
    axial_out, axial_in, edge_out, edge_in, mirror_out, mirror_in, mirror_mod,
    extra_out, extra_in, extra_own, section, modulated, near_out, near_in, far_out, far_in, message, from_edges, compact,
    load_sem, send_sem, recv_sem, go_sem,
):
    ax = lax.axis_index("ax")
    az = lax.axis_index("az")
    ax_count = lax.axis_size("ax")
    right = lax.rem(az + 1, SECTORS)
    left = lax.rem(az + SECTORS - 1, SECTORS)
    across = lax.rem(az + 2, SECTORS)
    has_low = ax > 0
    has_high = ax < ax_count - 1

    barrier = pltpu.get_barrier_semaphore()
    for sector in (right, left):
        pl.semaphore_signal(barrier, inc=1, device_id=(ax, sector), device_id_type=MESH)

    @pl.when(has_low)
    def _():
        pl.semaphore_signal(barrier, inc=1, device_id=(ax - 1, az), device_id_type=MESH)

    @pl.when(has_high)
    def _():
        pl.semaphore_signal(barrier, inc=1, device_id=(ax + 1, az), device_id_type=MESH)

    load_cells = pltpu.make_async_copy(conserved, cells, load_sem.at[0])
    load_table = pltpu.make_async_copy(tables, table, load_sem.at[1])
    load_mode = pltpu.make_async_copy(modes, mode, load_sem.at[2])
    load_count = pltpu.make_async_copy(counts, count, load_sem.at[3])
    load_mode.start()
    load_count.start()
    load_cells.start()
    load_table.start()

    def tab(name):
        low, high = SPANS[name]
        return table[low:high]

    row = lax.broadcasted_iota(jnp.int32, (8, WIDTH), 0)
    lane = lax.broadcasted_iota(jnp.int32, (8, WIDTH), 1)
    lines_all = FIELDS * LINES
    for low, high in ((NEAR_ROWS, NEAR_PAD), (NEAR_PAD + NEAR_ROWS, 2 * NEAR_PAD), (2 * NEAR_PAD + FAR_ROWS, MESSAGE_ROWS)):
        message[low:high] = jnp.zeros((high - low, lines_all), jnp.float32)
    load_mode.wait()
    load_count.wait()
    mode_tiles = []
    for tile in range(ROWS // 8):
        value = jnp.zeros((8, WIDTH), jnp.int32)
        for j in range(8):
            value = jnp.where(row == j, mode[tile * 8 + j], value)
        mode_tiles.append(value)
    ring_modes = jnp.concatenate(mode_tiles, axis=0)
    inner_modes = jnp.zeros((8, WIDTH), jnp.int32)
    for j in range(4):
        inner_modes = jnp.where((row & 3) == j, mode[j], inner_modes)
    line_modes = jnp.zeros((8, WIDTH), jnp.int32)
    for j in range(ROWS):
        line_modes = jnp.where((lane & (ROWS - 1)) == j, mode[j], line_modes)
    edge_c, edge_s = waves(line_modes, az * WIDTH + row + jnp.where(row < 4, -4, WIDTH - 4))
    wave_c, wave_s = sector_waves(ring_modes, az)
    inner_c, inner_s = sector_waves(inner_modes, az)
    across_c, across_s = sector_waves(inner_modes, across)
    harmonic = lane & (MODE_MOST - 1)
    base_weight = jnp.where(harmonic == 0, 1.0 / NT, 2.0 / NT).astype(jnp.float32)
    ring_harmonic = lax.broadcasted_iota(jnp.int32, (ROWS, WIDTH), 1) & (MODE_MOST - 1)
    ring_base = jnp.where(ring_harmonic == 0, 1.0 / NT, 2.0 / NT).astype(jnp.float32)
    ring_weight = jnp.where(ring_harmonic < ring_modes, ring_base, 0.0)
    inner_weight = jnp.where(harmonic < inner_modes, base_weight, 0.0)
    ring_row = lax.broadcasted_iota(jnp.int32, (ROWS, WIDTH), 0)
    per_radius = TIME_STEP / (ring_row.astype(jnp.float32) + 0.5)

    load_cells.wait()
    for x in range(STATIONS):
        s0, s1, s2, s3, s4 = (cells[x, c] for c in range(FIELDS))
        inverse = 1.0 / s0
        a = s1 * inverse
        b = s2 * inverse
        d = s3 * inverse
        p = GAS_FACTOR * (s4 - 0.5 * (s1 * a + s2 * b + s3 * d))
        e = s4 + p
        lines = pl.ds(x * ROWS, ROWS)
        flux_f[x, 0], flux_f[x, 1], flux_f[x, 2], flux_f[x, 3], flux_f[x, 4] = s1, s1 * a + p, s2 * a, s3 * a, a * e
        for c, value in enumerate((s2, s1 * b, s2 * b + p, s3 * b, b * e)):
            flux_g[c, lines] = value
        swirl_two = s2 * d
        swirl_three = s3 * d + p
        for c, value in enumerate((s3, s1 * d, swirl_two, swirl_three, d * e)):
            flux_h[c, lines] = value * (per_radius * (NT / (2.0 * math.pi)))
        for c, value in enumerate((s0, s1, s2 + per_radius * swirl_three, s3 - per_radius * swirl_two, s4)):
            section[c, lines] = value
    for c in range(FIELDS):
        for i in range(STATIONS):
            own = from_low = to_high = to_low = None
            for s in range(STATIONS):
                value = flux_f[s, c]
                if s != i:
                    weight = TIME_STEP * STENCIL[abs(s - i) - 1] * (-1.0 if s > i else 1.0)
                    own = weight * value if own is None else own + weight * value
                if s >= i:
                    term = TIME_STEP * STENCIL[3 + i - s] * value
                    to_high = term if to_high is None else to_high + term
                if s <= i:
                    term = -TIME_STEP * STENCIL[3 + s - i] * value
                    to_low = term if to_low is None else to_low + term
            section[c, pl.ds(i * ROWS, ROWS)] += own
            axial_out[1, i, c] = to_high
            axial_out[0, i, c] = to_low
            edge_weight = TIME_STEP * sum(STENCIL[i:])
            pl.when(jnp.logical_not(has_low))(
                functools.partial(store, axial_in, (0, i, c), edge_weight * flux_f[0, c])
            )
            edge_weight = -TIME_STEP * sum(STENCIL[3 - i :])
            pl.when(jnp.logical_not(has_high))(
                functools.partial(store, axial_in, (1, i, c), edge_weight * flux_f[3, c])
            )

    load_table.wait()
    edges = matmul(tab("edge"), flux_h[...].reshape(FIELDS * LINES, WIDTH), ((1,), (1,)))
    edge_out[0] = edges[0:4]
    edge_out[1] = edges[4:8]
    edge_waves = jnp.concatenate(
        [edges * jnp.concatenate([edge_c] * FIELDS, axis=1), edges * jnp.concatenate([edge_s] * FIELDS, axis=1)], axis=0
    )
    from_edges[...] = matmul(tab("source_edge")[:, 0:16], edge_waves)
    mirror_table = tab("mirror")
    for c in range(FIELDS):
        value = MIRROR_SIGNS[c] * matmul(mirror_table, flux_g[c])
        mirror_out[pl.ds(16 * c, 16)] = value
        for half in range(2):
            lines = pl.ds(16 * c + 8 * half, 8)
            mirror_mod[lines, 0:WIDTH] = value[8 * half : 8 * half + 8] * across_c
            mirror_mod[lines, WIDTH : 2 * WIDTH] = value[8 * half : 8 * half + 8] * across_s
    mirror_mod[80:128] = jnp.zeros((48, 2 * WIDTH), jnp.float32)
    sources = jnp.concatenate([tab("source_a"), tab("source_b")], axis=1)
    extra = matmul(sources, mirror_mod[...], ((1,), (1,)))
    extra_out[...] = extra[0 : 2 * NEAR_PAD]
    extra_own[...] = extra[2 * NEAR_PAD : 64]
    radial_table = tab("radial")
    swirl_table = tab("swirl")
    for c in range(FIELDS):
        section[c] += matmul(radial_table, flux_g[c]) + matmul(flux_h[c], swirl_table)

    def remote(source, target, slot, device):
        return pltpu.make_async_remote_copy(
            src_ref=source, dst_ref=target, send_sem=send_sem.at[slot], recv_sem=recv_sem.at[slot],
            device_id=device, device_id_type=MESH,
        )

    pl.semaphore_wait(barrier, 2 + has_low.astype(jnp.int32) + has_high.astype(jnp.int32))
    to_high = remote(axial_out.at[1], axial_in.at[0], 0, (ax + 1, az))
    to_low = remote(axial_out.at[0], axial_in.at[1], 1, (ax - 1, az))
    edge_left = remote(edge_out.at[0], edge_in.at[0], 2, (ax, left))
    edge_right = remote(edge_out.at[1], edge_in.at[1], 3, (ax, right))
    extra_left = remote(extra_out.at[0:NEAR_PAD], extra_in.at[0:NEAR_PAD], 5, (ax, left))
    extra_right = remote(
        extra_out.at[NEAR_PAD : 2 * NEAR_PAD], extra_in.at[NEAR_PAD : 2 * NEAR_PAD], 6, (ax, right)
    )
    mirror_copy = remote(mirror_out, mirror_in, 4, (ax, across))
    far_copy = remote(far_out, far_in, 7, (ax, across))
    near_right = remote(near_out.at[0], near_in.at[0], 8, (ax, right))
    near_left = remote(near_out.at[1], near_in.at[1], 9, (ax, left))
    for sector in (right, left):
        pl.semaphore_signal(go_sem, inc=1, device_id=(ax, sector), device_id_type=MESH)
    edge_left.start()
    edge_right.start()
    pl.when(has_high)(to_high.start)
    pl.when(has_low)(to_low.start)
    extra_left.start()
    extra_right.start()
    pl.semaphore_wait(go_sem, 2)
    mirror_copy.start()

    pl.when(has_high)(to_low_wait(remote(axial_out.at[1], axial_in.at[1], 1, (ax + 1, az))))
    pl.when(has_low)(to_low_wait(remote(axial_out.at[0], axial_in.at[0], 0, (ax - 1, az))))
    for c in range(FIELDS):
        for x in range(STATIONS):
            lines = pl.ds(x * ROWS, ROWS)
            value = section[c, lines] + axial_in[0, x, c] + axial_in[1, x, c]
            section[c, lines] = value
            modulated[pl.ds(c * LINES + x * ROWS, ROWS), 0:WIDTH] = value * wave_c
            modulated[pl.ds(c * LINES + x * ROWS, ROWS), WIDTH : 2 * WIDTH] = value * wave_s
    messages = matmul(sources, modulated[...], ((1,), (1,))) + from_edges[0:MESSAGE_ROWS]
    far_out[...] = messages[2 * NEAR_PAD : 2 * NEAR_PAD + FAR_ROWS]
    near_out[0] = messages[0:NEAR_ROWS]
    near_out[1] = messages[NEAR_PAD : NEAR_PAD + NEAR_ROWS]
    far_copy.start()
    mirror_copy.wait_send()
    near_right.start()
    near_left.start()

    edge_left.wait_recv()
    edge_right.wait_recv()
    edges = jnp.concatenate([edge_in[0], edge_in[1]], axis=0)
    place = tab("place")
    for c in range(FIELDS):
        section[c] += matmul(edges[:, c * LINES : (c + 1) * LINES], place, ((0,), (0,)))

    basis = tab("basis")
    for c in range(FIELDS):
        coefficients = matmul(section[c], basis)
        weighted = coefficients * jnp.concatenate([ring_weight] * STATIONS, axis=0)
        smoothed = matmul(weighted, basis, ((1,), (1,)))
        for x in range(STATIONS):
            modulated[pl.ds(c * LINES + x * ROWS, ROWS), 0:WIDTH] = smoothed[x * ROWS : (x + 1) * ROWS]

    part_row = lax.broadcasted_iota(jnp.int32, (64, 2 * WIDTH), 0)
    sign_left = jnp.where(az == 0, -1.0, 1.0)
    sign_right = jnp.where(az == SECTORS - 1, -1.0, 1.0)
    sign_across = jnp.where(az < 2, -1.0, 1.0)
    self_row = lax.broadcasted_iota(jnp.int32, (2 * NEAR_PAD, FIELDS * LINES), 0)
    from_edges[MESSAGE_ROWS : MESSAGE_ROWS + 2 * NEAR_PAD] = from_edges[
        MESSAGE_ROWS : MESSAGE_ROWS + 2 * NEAR_PAD
    ] * jnp.where(self_row < NEAR_PAD, sign_left, sign_right).astype(jnp.float32)
    signs = jnp.where(part_row < NEAR_PAD, sign_left, jnp.where(part_row < 2 * NEAR_PAD, sign_right, sign_across))
    targets = jnp.concatenate([tab("target_a"), tab("target_b")], axis=1) * signs.astype(jnp.float32)

    extra_left.wait_recv()
    extra_right.wait_recv()
    extra = jnp.concatenate([extra_in[...], extra_own[...]], axis=0)
    extra_field = matmul(extra, targets, ((0,), (0,)))
    mirror_copy.wait_recv()
    mirrored = mirror_in[...]
    weighted = matmul(mirrored, basis) * jnp.concatenate([inner_weight] * 10, axis=0)
    compact_smooth = matmul(weighted, basis, ((1,), (1,)))
    for c in range(FIELDS):
        for half in range(2):
            lines = pl.ds(16 * c + 8 * half, 8)
            low = 16 * c + 8 * half
            smooth = (
                compact_smooth[low : low + 8]
                + inner_s * extra_field[low : low + 8, 0:WIDTH]
                + inner_c * extra_field[low : low + 8, WIDTH : 2 * WIDTH]
            )
            limit = jnp.where(row < 4, count[2 * half], count[2 * half + 1])
            compact[lines] = jnp.where((row & 3) < limit, smooth, mirror_in[lines])

    far_copy.wait_recv()
    message[2 * NEAR_PAD : 2 * NEAR_PAD + FAR_ROWS] = far_in[...]
    near_right.wait_recv()
    message[0:NEAR_ROWS] = near_in[0] + from_edges[MESSAGE_ROWS : MESSAGE_ROWS + NEAR_ROWS]
    near_left.wait_recv()
    own_left = MESSAGE_ROWS + NEAR_PAD
    message[NEAR_PAD : NEAR_PAD + NEAR_ROWS] = near_in[1] + from_edges[own_left : own_left + NEAR_ROWS]
    for c in range(FIELDS):
        field = matmul(message[:, c * LINES : (c + 1) * LINES], targets, ((0,), (0,)))
        for x in range(STATIONS):
            low = x * ROWS
            smooth = (
                modulated[pl.ds(c * LINES + low, ROWS), 0:WIDTH]
                + wave_s * field[low : low + ROWS, 0:WIDTH]
                + wave_c * field[low : low + ROWS, WIDTH : 2 * WIDTH]
            )
            out[x, c] = jnp.where(ring_row < count[x], smooth, section[c, pl.ds(low, ROWS)])
            out[x, c, 0:4] += compact[pl.ds(16 * c + 4 * x, 4)]

    pl.when(has_high)(to_high.wait_send)
    pl.when(has_low)(to_low.wait_send)
    for copy in (edge_left, edge_right, extra_left, extra_right, far_copy, near_right, near_left):
        copy.wait_send()


def store(ref, index, value):
    ref[index] = value


def to_low_wait(copy):
    return copy.wait_recv


def per_device(conserved, cycle_modes, filtered_cycles):
    f32 = jnp.float32
    block = (STATIONS, FIELDS, ROWS, WIDTH)
    lines = FIELDS * LINES
    return pl.pallas_call(
        body,
        out_shape=jax.ShapeDtypeStruct(block, f32),
        in_specs=[
            pl.BlockSpec(memory_space=pltpu.HBM),
            pl.BlockSpec(memory_space=pltpu.HBM),
            pl.BlockSpec(memory_space=pltpu.HBM),
            pl.BlockSpec(memory_space=pltpu.HBM),
        ],
        out_specs=pl.BlockSpec(memory_space=pltpu.VMEM),
        scratch_shapes=[
            pltpu.VMEM(block, f32),
            pltpu.VMEM(TABLES.shape, f32),
            pltpu.SMEM((ROWS,), jnp.int32),
            pltpu.SMEM((STATIONS,), jnp.int32),
            pltpu.VMEM(block, f32),
            pltpu.VMEM((FIELDS, LINES, WIDTH), f32),
            pltpu.VMEM((FIELDS, LINES, WIDTH), f32),
            pltpu.VMEM((2,) + block, f32),
            pltpu.VMEM((2,) + block, f32),
            pltpu.VMEM((2, 4, lines), f32),
            pltpu.VMEM((2, 4, lines), f32),
            pltpu.VMEM((80, WIDTH), f32),
            pltpu.VMEM((80, WIDTH), f32),
            pltpu.VMEM((128, 2 * WIDTH), f32),
            pltpu.VMEM((2 * NEAR_PAD, WIDTH), f32),
            pltpu.VMEM((2 * NEAR_PAD, WIDTH), f32),
            pltpu.VMEM((16, WIDTH), f32),
            pltpu.VMEM((FIELDS, LINES, WIDTH), f32),
            pltpu.VMEM((lines, 2 * WIDTH), f32),
            pltpu.VMEM((2, NEAR_ROWS, lines), f32),
            pltpu.VMEM((2, NEAR_ROWS, lines), f32),
            pltpu.VMEM((FAR_ROWS, lines), f32),
            pltpu.VMEM((FAR_ROWS, lines), f32),
            pltpu.VMEM((MESSAGE_ROWS, lines), f32),
            pltpu.VMEM((2 * MESSAGE_ROWS, lines), f32),
            pltpu.VMEM((80, WIDTH), f32),
            pltpu.SemaphoreType.DMA((4,)),
            pltpu.SemaphoreType.DMA((10,)),
            pltpu.SemaphoreType.DMA((10,)),
            pltpu.SemaphoreType.REGULAR,
        ],
        compiler_params=pltpu.CompilerParams(
            collective_id=0, has_side_effects=True, vmem_limit_bytes=60 * 1024 * 1024
        ),
    )(conserved, jnp.asarray(TABLES), cycle_modes, filtered_cycles)


def solution(mesh):
    placed = (P("ax", None, None, "az"), P(), P("ax"))
    return jax.shard_map(
        per_device, mesh=mesh, in_specs=placed, out_specs=P("ax", None, None, "az"), check_vma=False
    )
```

```python
import functools
import math

import jax
import jax.numpy as jnp
import numpy as np
from jax import lax
from jax.experimental import pallas as pl
from jax.experimental.pallas import tpu as pltpu
from jax.sharding import PartitionSpec as P

NT = 512
NRF = 32
MODE_MOST = 64
STENCIL = (0.8, -0.2, 4.0 / 105.0, -1.0 / 280.0)
GAS_FACTOR = 0.4
TIME_STEP = 0.1

SECTORS = 4
WIDTH = NT // SECTORS
STATIONS = 4
FIELDS = 5
ROWS = 32
LINES = STATIONS * ROWS
NEAR = 10
FAR = 5
MESH = pl.DeviceIdType.MESH
EXACT = lax.Precision.HIGHEST
MIRROR_SIGNS = (1.0, 1.0, -1.0, -1.0, 1.0)


def kernel_factors(distance, rank, sources):
    gap = WIDTH * distance + np.arange(WIDTH)[:, None] - sources[None, :]
    left, values, right = np.linalg.svd(1.0 / np.sin(np.pi * gap / NT))
    root = np.sqrt(values[:rank])
    return (left[:, :rank] * root).T, right[:rank] * root[:, None]


NEAR_ROWS = 2 * NEAR
FAR_ROWS = 2 * FAR
NEAR_PAD = 24
MESSAGE_ROWS = 64


def build_tables():
    parts = {}
    radius = np.arange(ROWS) + 0.5
    ring = np.zeros((ROWS, ROWS))
    mirror = np.zeros((4, ROWS))
    for row in range(ROWS):
        for k, weight in enumerate(STENCIL, 1):
            ring[row, min(row + k, ROWS - 1)] -= TIME_STEP * weight * (row + k + 0.5) / radius[row]
            below = row - k
            if below >= 0:
                ring[row, below] += TIME_STEP * weight * (below + 0.5) / radius[row]
            else:
                mirror[row, -1 - below] += TIME_STEP * weight * (-below - 0.5) / radius[row]
    parts["radial"] = np.kron(np.eye(STATIONS), ring)
    parts["mirror"] = np.kron(np.eye(STATIONS), mirror)
    swirl = np.zeros((WIDTH, WIDTH))
    edge = np.zeros((8, WIDTH))
    place = np.zeros((8, WIDTH))
    for cell in range(-4, WIDTH + 4):
        for k, weight in enumerate(STENCIL, 1):
            for source, value in ((cell + k, -weight), (cell - k, weight)):
                if 0 <= source < WIDTH:
                    if cell < 0:
                        edge[cell + 4, source] += value
                    elif cell >= WIDTH:
                        edge[cell - WIDTH + 4, source] += value
                    else:
                        swirl[source, cell] += value
    for cell in range(4):
        place[cell, WIDTH - 4 + cell] = 1.0
        place[4 + cell, cell] = 1.0
    parts["swirl"] = swirl
    parts["edge"] = edge
    parts["place"] = place
    angle = 2.0 * np.pi / NT * np.arange(WIDTH)[:, None] * np.arange(MODE_MOST)[None, :]
    parts["basis"] = np.concatenate([np.cos(angle), np.sin(angle)], axis=1)
    source_a = np.zeros((64, WIDTH))
    source_b = np.zeros((64, WIDTH))
    target_a = np.zeros((64, WIDTH))
    target_b = np.zeros((64, WIDTH))
    source_edge = np.zeros((2 * MESSAGE_ROWS, WIDTH))
    for distance, rank, first, low, high in (
        (1, NEAR, 0, -4, WIDTH),
        (-1, NEAR, NEAR_PAD, 0, WIDTH + 4),
        (2, FAR, 2 * NEAR_PAD, -4, WIDTH + 4),
    ):
        target, source = kernel_factors(distance, rank, np.arange(low, high))
        own = source[:, -low : WIDTH - low]
        for wave, (into, out_of, half) in enumerate(((source_a, target_a, 1.0 / NT), (source_b, target_b, -1.0 / NT))):
            rows = slice(first + wave * rank, first + (wave + 1) * rank)
            back = slice(MESSAGE_ROWS + rows.start, MESSAGE_ROWS + rows.stop)
            into[rows] = own
            out_of[rows] = half * target
            if low < 0:
                source_edge[rows, 8 * wave : 8 * wave + 4] = source[:, 0:4]
            if high > WIDTH:
                source_edge[rows, 8 * wave + 4 : 8 * wave + 8] = source[:, -4:]
            if distance == 1:
                source_edge[back, 8 * wave : 8 * wave + 4] = own[:, -4:]
            if distance == -1:
                source_edge[back, 8 * wave + 4 : 8 * wave + 8] = own[:, 0:4]
    parts["source_a"] = source_a
    parts["source_b"] = source_b
    parts["source_edge"] = source_edge
    parts["target_a"] = target_a
    parts["target_b"] = target_b
    spans, blocks, start = {}, [], 0
    for name, block in parts.items():
        spans[name] = (start, start + block.shape[0])
        start += block.shape[0]
        blocks.append(block)
    return np.concatenate(blocks, axis=0).astype(np.float32), spans


TABLES, SPANS = build_tables()


def matmul(left, right, dims=((1,), (0,))):
    return lax.dot_general(left, right, (dims, ((), ())), precision=EXACT, preferred_element_type=jnp.float32)


def sector_waves(modes, sector):
    return waves(modes, lax.broadcasted_iota(jnp.int32, modes.shape, 1) + sector * WIDTH)


def waves(modes, cell):
    turn = ((2 * modes - 1) * cell) & (2 * NT - 1)
    angle = turn.astype(jnp.float32) * (math.pi / NT)
    return jnp.cos(angle), jnp.sin(angle)


def body(
    conserved, tables, modes, counts, out,
    cells, table, mode, count, flux_f, flux_g, flux_h,
    axial_out, axial_in, edge_out, edge_in, mirror_out, mirror_in, mirror_mod,
    extra_out, extra_in, extra_own, section, modulated, near_out, near_in, far_out, far_in, message, from_edges, compact,
    load_sem, send_sem, recv_sem, go_sem,
):
    ax = lax.axis_index("ax")
    az = lax.axis_index("az")
    ax_count = lax.axis_size("ax")
    right = lax.rem(az + 1, SECTORS)
    left = lax.rem(az + SECTORS - 1, SECTORS)
    across = lax.rem(az + 2, SECTORS)
    has_low = ax > 0
    has_high = ax < ax_count - 1

    barrier = pltpu.get_barrier_semaphore()
    for sector in (right, left):
        pl.semaphore_signal(barrier, inc=1, device_id=(ax, sector), device_id_type=MESH)

    @pl.when(has_low)
    def _():
        pl.semaphore_signal(barrier, inc=1, device_id=(ax - 1, az), device_id_type=MESH)

    @pl.when(has_high)
    def _():
        pl.semaphore_signal(barrier, inc=1, device_id=(ax + 1, az), device_id_type=MESH)

    load_cells = pltpu.make_async_copy(conserved, cells, load_sem.at[0])
    load_table = pltpu.make_async_copy(tables, table, load_sem.at[1])
    load_mode = pltpu.make_async_copy(modes, mode, load_sem.at[2])
    load_count = pltpu.make_async_copy(counts, count, load_sem.at[3])
    load_mode.start()
    load_count.start()
    load_cells.start()
    load_table.start()

    def tab(name):
        low, high = SPANS[name]
        return table[low:high]

    row = lax.broadcasted_iota(jnp.int32, (8, WIDTH), 0)
    lane = lax.broadcasted_iota(jnp.int32, (8, WIDTH), 1)
    lines_all = FIELDS * LINES
    for low, high in ((NEAR_ROWS, NEAR_PAD), (NEAR_PAD + NEAR_ROWS, 2 * NEAR_PAD), (2 * NEAR_PAD + FAR_ROWS, MESSAGE_ROWS)):
        message[low:high] = jnp.zeros((high - low, lines_all), jnp.float32)
    load_mode.wait()
    load_count.wait()
    mode_tiles = []
    for tile in range(ROWS // 8):
        value = jnp.zeros((8, WIDTH), jnp.int32)
        for j in range(8):
            value = jnp.where(row == j, mode[tile * 8 + j], value)
        mode_tiles.append(value)
    ring_modes = jnp.concatenate(mode_tiles, axis=0)
    inner_modes = jnp.zeros((8, WIDTH), jnp.int32)
    for j in range(4):
        inner_modes = jnp.where((row & 3) == j, mode[j], inner_modes)
    line_modes = jnp.zeros((8, WIDTH), jnp.int32)
    for j in range(ROWS):
        line_modes = jnp.where((lane & (ROWS - 1)) == j, mode[j], line_modes)
    edge_c, edge_s = waves(line_modes, az * WIDTH + row + jnp.where(row < 4, -4, WIDTH - 4))
    wave_c, wave_s = sector_waves(ring_modes, az)
    inner_c, inner_s = sector_waves(inner_modes, az)
    across_c, across_s = sector_waves(inner_modes, across)
    harmonic = lane & (MODE_MOST - 1)
    base_weight = jnp.where(harmonic == 0, 1.0 / NT, 2.0 / NT).astype(jnp.float32)
    ring_harmonic = lax.broadcasted_iota(jnp.int32, (ROWS, WIDTH), 1) & (MODE_MOST - 1)
    ring_base = jnp.where(ring_harmonic == 0, 1.0 / NT, 2.0 / NT).astype(jnp.float32)
    ring_weight = jnp.where(ring_harmonic < ring_modes, ring_base, 0.0)
    inner_weight = jnp.where(harmonic < inner_modes, base_weight, 0.0)
    ring_row = lax.broadcasted_iota(jnp.int32, (ROWS, WIDTH), 0)
    per_radius = TIME_STEP / (ring_row.astype(jnp.float32) + 0.5)

    load_cells.wait()
    for x in range(STATIONS):
        s0, s1, s2, s3, s4 = (cells[x, c] for c in range(FIELDS))
        inverse = 1.0 / s0
        a = s1 * inverse
        b = s2 * inverse
        d = s3 * inverse
        p = GAS_FACTOR * (s4 - 0.5 * (s1 * a + s2 * b + s3 * d))
        e = s4 + p
        lines = pl.ds(x * ROWS, ROWS)
        flux_f[x, 0], flux_f[x, 1], flux_f[x, 2], flux_f[x, 3], flux_f[x, 4] = s1, s1 * a + p, s2 * a, s3 * a, a * e
        for c, value in enumerate((s2, s1 * b, s2 * b + p, s3 * b, b * e)):
            flux_g[c, lines] = value
        swirl_two = s2 * d
        swirl_three = s3 * d + p
        for c, value in enumerate((s3, s1 * d, swirl_two, swirl_three, d * e)):
            flux_h[c, lines] = value * (per_radius * (NT / (2.0 * math.pi)))
        for c, value in enumerate((s0, s1, s2 + per_radius * swirl_three, s3 - per_radius * swirl_two, s4)):
            section[c, lines] = value
    for c in range(FIELDS):
        for i in range(STATIONS):
            own = from_low = to_high = to_low = None
            for s in range(STATIONS):
                value = flux_f[s, c]
                if s != i:
                    weight = TIME_STEP * STENCIL[abs(s - i) - 1] * (-1.0 if s > i else 1.0)
                    own = weight * value if own is None else own + weight * value
                if s >= i:
                    term = TIME_STEP * STENCIL[3 + i - s] * value
                    to_high = term if to_high is None else to_high + term
                if s <= i:
                    term = -TIME_STEP * STENCIL[3 + s - i] * value
                    to_low = term if to_low is None else to_low + term
            section[c, pl.ds(i * ROWS, ROWS)] += own
            axial_out[1, i, c] = to_high
            axial_out[0, i, c] = to_low
            edge_weight = TIME_STEP * sum(STENCIL[i:])
            pl.when(jnp.logical_not(has_low))(
                functools.partial(store, axial_in, (0, i, c), edge_weight * flux_f[0, c])
            )
            edge_weight = -TIME_STEP * sum(STENCIL[3 - i :])
            pl.when(jnp.logical_not(has_high))(
                functools.partial(store, axial_in, (1, i, c), edge_weight * flux_f[3, c])
            )

    load_table.wait()
    edges = matmul(tab("edge"), flux_h[...].reshape(FIELDS * LINES, WIDTH), ((1,), (1,)))
    pack(edge_out, edges[0:4], 0)
    pack(edge_out, edges[4:8], 1)
    edge_waves = jnp.concatenate(
        [edges * jnp.concatenate([edge_c] * FIELDS, axis=1), edges * jnp.concatenate([edge_s] * FIELDS, axis=1)], axis=0
    )
    from_edges[...] = matmul(tab("source_edge")[:, 0:16], edge_waves)
    mirror_table = tab("mirror")
    for c in range(FIELDS):
        value = MIRROR_SIGNS[c] * matmul(mirror_table, flux_g[c])
        mirror_out[pl.ds(16 * c, 16)] = value
        for half in range(2):
            lines = pl.ds(16 * c + 8 * half, 8)
            mirror_mod[lines, 0:WIDTH] = value[8 * half : 8 * half + 8] * across_c
            mirror_mod[lines, WIDTH : 2 * WIDTH] = value[8 * half : 8 * half + 8] * across_s
    mirror_mod[80:128] = jnp.zeros((48, 2 * WIDTH), jnp.float32)
    sources = jnp.concatenate([tab("source_a"), tab("source_b")], axis=1)
    extra = matmul(sources, mirror_mod[...], ((1,), (1,)))
    extra_out[0] = extra[0:NEAR_ROWS]
    extra_out[1] = extra[NEAR_PAD : NEAR_PAD + NEAR_ROWS]
    extra_own[...] = extra[2 * NEAR_PAD : 64]
    radial_table = tab("radial")
    swirl_table = tab("swirl")
    for c in range(FIELDS):
        section[c] += matmul(radial_table, flux_g[c]) + matmul(flux_h[c], swirl_table)

    def remote(source, target, slot, device):
        return pltpu.make_async_remote_copy(
            src_ref=source, dst_ref=target, send_sem=send_sem.at[slot], recv_sem=recv_sem.at[slot],
            device_id=device, device_id_type=MESH,
        )

    pl.semaphore_wait(barrier, 2 + has_low.astype(jnp.int32) + has_high.astype(jnp.int32))
    to_high = remote(axial_out.at[1], axial_in.at[0], 0, (ax + 1, az))
    to_low = remote(axial_out.at[0], axial_in.at[1], 1, (ax - 1, az))
    edge_left = remote(edge_out.at[0], edge_in.at[0], 2, (ax, left))
    edge_right = remote(edge_out.at[1], edge_in.at[1], 3, (ax, right))
    extra_left = remote(extra_out.at[0], extra_in.at[0], 5, (ax, left))
    extra_right = remote(extra_out.at[1], extra_in.at[1], 6, (ax, right))
    mirror_copy = remote(mirror_out, mirror_in, 4, (ax, across))
    far_copy = remote(far_out.at[0], far_in.at[0], 7, (ax, across))
    near_right = remote(near_out.at[0], near_in.at[0], 8, (ax, right))
    near_left = remote(near_out.at[1], near_in.at[1], 9, (ax, left))
    for sector in (right, left):
        pl.semaphore_signal(go_sem, inc=1, device_id=(ax, sector), device_id_type=MESH)
    edge_left.start()
    edge_right.start()
    pl.when(has_high)(to_high.start)
    pl.when(has_low)(to_low.start)
    extra_left.start()
    extra_right.start()
    pl.semaphore_wait(go_sem, 2)
    mirror_copy.start()

    pl.when(has_high)(to_low_wait(remote(axial_out.at[1], axial_in.at[1], 1, (ax + 1, az))))
    pl.when(has_low)(to_low_wait(remote(axial_out.at[0], axial_in.at[0], 0, (ax - 1, az))))
    for c in range(FIELDS):
        for x in range(STATIONS):
            lines = pl.ds(x * ROWS, ROWS)
            value = section[c, lines] + axial_in[0, x, c] + axial_in[1, x, c]
            section[c, lines] = value
            modulated[pl.ds(c * LINES + x * ROWS, ROWS), 0:WIDTH] = value * wave_c
            modulated[pl.ds(c * LINES + x * ROWS, ROWS), WIDTH : 2 * WIDTH] = value * wave_s
    messages = matmul(sources, modulated[...], ((1,), (1,))) + from_edges[0:MESSAGE_ROWS]
    pack(far_out, messages[2 * NEAR_PAD : 2 * NEAR_PAD + FAR_ROWS], 0)
    pack(near_out, messages[0:NEAR_ROWS], 0)
    pack(near_out, messages[NEAR_PAD : NEAR_PAD + NEAR_ROWS], 1)
    far_copy.start()
    mirror_copy.wait_send()
    near_right.start()
    near_left.start()

    edge_left.wait_recv()
    edge_right.wait_recv()
    edges = jnp.concatenate([unpack(edge_in, 4, 0), unpack(edge_in, 4, 1)], axis=0)
    place = tab("place")
    for c in range(FIELDS):
        section[c] += matmul(edges[:, c * LINES : (c + 1) * LINES], place, ((0,), (0,)))

    basis = tab("basis")
    for c in range(FIELDS):
        coefficients = matmul(section[c], basis)
        weighted = coefficients * jnp.concatenate([ring_weight] * STATIONS, axis=0)
        smoothed = matmul(weighted, basis, ((1,), (1,)))
        for x in range(STATIONS):
            modulated[pl.ds(c * LINES + x * ROWS, ROWS), 0:WIDTH] = smoothed[x * ROWS : (x + 1) * ROWS]

    part_row = lax.broadcasted_iota(jnp.int32, (64, 2 * WIDTH), 0)
    sign_left = jnp.where(az == 0, -1.0, 1.0)
    sign_right = jnp.where(az == SECTORS - 1, -1.0, 1.0)
    sign_across = jnp.where(az < 2, -1.0, 1.0)
    self_row = lax.broadcasted_iota(jnp.int32, (2 * NEAR_PAD, FIELDS * LINES), 0)
    from_edges[MESSAGE_ROWS : MESSAGE_ROWS + 2 * NEAR_PAD] = from_edges[
        MESSAGE_ROWS : MESSAGE_ROWS + 2 * NEAR_PAD
    ] * jnp.where(self_row < NEAR_PAD, sign_left, sign_right).astype(jnp.float32)
    signs = jnp.where(part_row < NEAR_PAD, sign_left, jnp.where(part_row < 2 * NEAR_PAD, sign_right, sign_across))
    targets = jnp.concatenate([tab("target_a"), tab("target_b")], axis=1) * signs.astype(jnp.float32)

    extra_left.wait_recv()
    extra_right.wait_recv()
    fill = jnp.zeros((NEAR_PAD - NEAR_ROWS, WIDTH), jnp.float32)
    extra = jnp.concatenate([extra_in[0], fill, extra_in[1], fill, extra_own[...]], axis=0)
    extra_field = matmul(extra, targets, ((0,), (0,)))
    mirror_copy.wait_recv()
    mirrored = mirror_in[...]
    weighted = matmul(mirrored, basis) * jnp.concatenate([inner_weight] * 10, axis=0)
    compact_smooth = matmul(weighted, basis, ((1,), (1,)))
    for c in range(FIELDS):
        for half in range(2):
            lines = pl.ds(16 * c + 8 * half, 8)
            low = 16 * c + 8 * half
            smooth = (
                compact_smooth[low : low + 8]
                + inner_s * extra_field[low : low + 8, 0:WIDTH]
                + inner_c * extra_field[low : low + 8, WIDTH : 2 * WIDTH]
            )
            limit = jnp.where(row < 4, count[2 * half], count[2 * half + 1])
            compact[lines] = jnp.where((row & 3) < limit, smooth, mirror_in[lines])

    far_copy.wait_recv()
    message[2 * NEAR_PAD : 2 * NEAR_PAD + FAR_ROWS] = unpack(far_in, FAR_ROWS, 0)
    near_right.wait_recv()
    message[0:NEAR_ROWS] = unpack(near_in, NEAR_ROWS, 0) + from_edges[MESSAGE_ROWS : MESSAGE_ROWS + NEAR_ROWS]
    near_left.wait_recv()
    own_left = MESSAGE_ROWS + NEAR_PAD
    message[NEAR_PAD : NEAR_PAD + NEAR_ROWS] = unpack(near_in, NEAR_ROWS, 1) + from_edges[own_left : own_left + NEAR_ROWS]
    for c in range(FIELDS):
        field = matmul(message[:, c * LINES : (c + 1) * LINES], targets, ((0,), (0,)))
        for x in range(STATIONS):
            low = x * ROWS
            smooth = (
                modulated[pl.ds(c * LINES + low, ROWS), 0:WIDTH]
                + wave_s * field[low : low + ROWS, 0:WIDTH]
                + wave_c * field[low : low + ROWS, WIDTH : 2 * WIDTH]
            )
            out[x, c] = jnp.where(ring_row < count[x], smooth, section[c, pl.ds(low, ROWS)])
            out[x, c, 0:4] += compact[pl.ds(16 * c + 4 * x, 4)]

    pl.when(has_high)(to_high.wait_send)
    pl.when(has_low)(to_low.wait_send)
    for copy in (edge_left, edge_right, extra_left, extra_right, far_copy, near_right, near_left):
        copy.wait_send()


def pack(ref, value, slot):
    rows = value.shape[0]
    for c in range(FIELDS):
        ref[slot, c * rows : (c + 1) * rows] = value[:, c * LINES : (c + 1) * LINES]


def unpack(ref, rows, slot):
    return jnp.concatenate([ref[slot, c * rows : (c + 1) * rows] for c in range(FIELDS)], axis=1)


def store(ref, index, value):
    ref[index] = value


def to_low_wait(copy):
    return copy.wait_recv


def per_device(conserved, cycle_modes, filtered_cycles):
    f32 = jnp.float32
    block = (STATIONS, FIELDS, ROWS, WIDTH)
    lines = FIELDS * LINES
    return pl.pallas_call(
        body,
        out_shape=jax.ShapeDtypeStruct(block, f32),
        in_specs=[
            pl.BlockSpec(memory_space=pltpu.HBM),
            pl.BlockSpec(memory_space=pltpu.HBM),
            pl.BlockSpec(memory_space=pltpu.HBM),
            pl.BlockSpec(memory_space=pltpu.HBM),
        ],
        out_specs=pl.BlockSpec(memory_space=pltpu.VMEM),
        scratch_shapes=[
            pltpu.VMEM(block, f32),
            pltpu.VMEM(TABLES.shape, f32),
            pltpu.SMEM((ROWS,), jnp.int32),
            pltpu.SMEM((STATIONS,), jnp.int32),
            pltpu.VMEM(block, f32),
            pltpu.VMEM((FIELDS, LINES, WIDTH), f32),
            pltpu.VMEM((FIELDS, LINES, WIDTH), f32),
            pltpu.VMEM((2,) + block, f32),
            pltpu.VMEM((2,) + block, f32),
            pltpu.VMEM((2, FIELDS * 4, LINES), f32),
            pltpu.VMEM((2, FIELDS * 4, LINES), f32),
            pltpu.VMEM((80, WIDTH), f32),
            pltpu.VMEM((80, WIDTH), f32),
            pltpu.VMEM((128, 2 * WIDTH), f32),
            pltpu.VMEM((2, NEAR_ROWS, WIDTH), f32),
            pltpu.VMEM((2, NEAR_ROWS, WIDTH), f32),
            pltpu.VMEM((16, WIDTH), f32),
            pltpu.VMEM((FIELDS, LINES, WIDTH), f32),
            pltpu.VMEM((lines, 2 * WIDTH), f32),
            pltpu.VMEM((2, FIELDS * NEAR_ROWS, LINES), f32),
            pltpu.VMEM((2, FIELDS * NEAR_ROWS, LINES), f32),
            pltpu.VMEM((1, FIELDS * FAR_ROWS, LINES), f32),
            pltpu.VMEM((1, FIELDS * FAR_ROWS, LINES), f32),
            pltpu.VMEM((MESSAGE_ROWS, lines), f32),
            pltpu.VMEM((2 * MESSAGE_ROWS, lines), f32),
            pltpu.VMEM((80, WIDTH), f32),
            pltpu.SemaphoreType.DMA((4,)),
            pltpu.SemaphoreType.DMA((10,)),
            pltpu.SemaphoreType.DMA((10,)),
            pltpu.SemaphoreType.REGULAR,
        ],
        compiler_params=pltpu.CompilerParams(
            collective_id=0, has_side_effects=True, vmem_limit_bytes=60 * 1024 * 1024
        ),
    )(conserved, jnp.asarray(TABLES), cycle_modes, filtered_cycles)


def solution(mesh):
    placed = (P("ax", None, None, "az"), P(), P("ax"))
    return jax.shard_map(
        per_device, mesh=mesh, in_specs=placed, out_specs=P("ax", None, None, "az"), check_vma=False
    )
```

```python
import functools
import math

import jax
import jax.numpy as jnp
import numpy as np
from jax import lax
from jax.experimental import pallas as pl
from jax.experimental.pallas import tpu as pltpu
from jax.sharding import PartitionSpec as P

NT = 512
NRF = 32
MODE_MOST = 64
STENCIL = (0.8, -0.2, 4.0 / 105.0, -1.0 / 280.0)
GAS_FACTOR = 0.4
TIME_STEP = 0.1

SECTORS = 4
WIDTH = NT // SECTORS
STATIONS = 4
FIELDS = 5
ROWS = 32
LINES = STATIONS * ROWS
NEAR = 10
FAR = 5
MESH = pl.DeviceIdType.MESH
EXACT = lax.Precision.HIGHEST
MIRROR_SIGNS = (1.0, 1.0, -1.0, -1.0, 1.0)


def kernel_factors(distance, rank, sources):
    gap = WIDTH * distance + np.arange(WIDTH)[:, None] - sources[None, :]
    left, values, right = np.linalg.svd(1.0 / np.sin(np.pi * gap / NT))
    root = np.sqrt(values[:rank])
    return (left[:, :rank] * root).T, right[:rank] * root[:, None]


NEAR_ROWS = 2 * NEAR
FAR_ROWS = 2 * FAR
NEAR_PAD = 24
MESSAGE_ROWS = 64


def build_tables():
    parts = {}
    radius = np.arange(ROWS) + 0.5
    ring = np.zeros((ROWS, ROWS))
    mirror = np.zeros((4, ROWS))
    for row in range(ROWS):
        for k, weight in enumerate(STENCIL, 1):
            ring[row, min(row + k, ROWS - 1)] -= TIME_STEP * weight * (row + k + 0.5) / radius[row]
            below = row - k
            if below >= 0:
                ring[row, below] += TIME_STEP * weight * (below + 0.5) / radius[row]
            else:
                mirror[row, -1 - below] += TIME_STEP * weight * (-below - 0.5) / radius[row]
    parts["radial"] = np.kron(np.eye(STATIONS), ring)
    parts["mirror"] = np.kron(np.eye(STATIONS), mirror)
    swirl = np.zeros((WIDTH, WIDTH))
    edge = np.zeros((8, WIDTH))
    place = np.zeros((8, WIDTH))
    for cell in range(-4, WIDTH + 4):
        for k, weight in enumerate(STENCIL, 1):
            for source, value in ((cell + k, -weight), (cell - k, weight)):
                if 0 <= source < WIDTH:
                    if cell < 0:
                        edge[cell + 4, source] += value
                    elif cell >= WIDTH:
                        edge[cell - WIDTH + 4, source] += value
                    else:
                        swirl[source, cell] += value
    for cell in range(4):
        place[cell, WIDTH - 4 + cell] = 1.0
        place[4 + cell, cell] = 1.0
    parts["swirl"] = swirl
    parts["edge"] = edge
    parts["place"] = place
    angle = 2.0 * np.pi / NT * np.arange(WIDTH)[:, None] * np.arange(MODE_MOST)[None, :]
    parts["basis"] = np.concatenate([np.cos(angle), np.sin(angle)], axis=1)
    source_a = np.zeros((64, WIDTH))
    source_b = np.zeros((64, WIDTH))
    target_a = np.zeros((64, WIDTH))
    target_b = np.zeros((64, WIDTH))
    source_edge = np.zeros((2 * MESSAGE_ROWS, WIDTH))
    for distance, rank, first, low, high in (
        (1, NEAR, 0, -4, WIDTH),
        (-1, NEAR, NEAR_PAD, 0, WIDTH + 4),
        (2, FAR, 2 * NEAR_PAD, -4, WIDTH + 4),
    ):
        target, source = kernel_factors(distance, rank, np.arange(low, high))
        own = source[:, -low : WIDTH - low]
        for wave, (into, out_of, half) in enumerate(((source_a, target_a, 1.0 / NT), (source_b, target_b, -1.0 / NT))):
            rows = slice(first + wave * rank, first + (wave + 1) * rank)
            back = slice(MESSAGE_ROWS + rows.start, MESSAGE_ROWS + rows.stop)
            into[rows] = own
            out_of[rows] = half * target
            if low < 0:
                source_edge[rows, 8 * wave : 8 * wave + 4] = source[:, 0:4]
            if high > WIDTH:
                source_edge[rows, 8 * wave + 4 : 8 * wave + 8] = source[:, -4:]
            if distance == 1:
                source_edge[back, 8 * wave : 8 * wave + 4] = own[:, -4:]
            if distance == -1:
                source_edge[back, 8 * wave + 4 : 8 * wave + 8] = own[:, 0:4]
    parts["source_a"] = source_a
    parts["source_b"] = source_b
    parts["source_edge"] = source_edge
    parts["target_a"] = target_a
    parts["target_b"] = target_b
    spans, blocks, start = {}, [], 0
    for name, block in parts.items():
        spans[name] = (start, start + block.shape[0])
        start += block.shape[0]
        blocks.append(block)
    return np.concatenate(blocks, axis=0).astype(np.float32), spans


TABLES, SPANS = build_tables()


def matmul(left, right, dims=((1,), (0,))):
    return lax.dot_general(left, right, (dims, ((), ())), precision=EXACT, preferred_element_type=jnp.float32)


def sector_waves(modes, sector):
    return waves(modes, lax.broadcasted_iota(jnp.int32, modes.shape, 1) + sector * WIDTH)


def waves(modes, cell):
    turn = ((2 * modes - 1) * cell) & (2 * NT - 1)
    angle = turn.astype(jnp.float32) * (math.pi / NT)
    return jnp.cos(angle), jnp.sin(angle)


def body(
    conserved, tables, modes, counts, out,
    cells, table, mode, count, flux_f, flux_g, flux_h,
    axial_out, axial_in, edge_out, edge_in, mirror_out, mirror_in, mirror_mod,
    extra_out, extra_in, extra_own, section, modulated, near_out, near_in, far_out, far_in, message, from_edges, compact,
    load_sem, send_sem, recv_sem, go_sem,
):
    ax = lax.axis_index("ax")
    az = lax.axis_index("az")
    ax_count = lax.axis_size("ax")
    right = lax.rem(az + 1, SECTORS)
    left = lax.rem(az + SECTORS - 1, SECTORS)
    across = lax.rem(az + 2, SECTORS)
    has_low = ax > 0
    has_high = ax < ax_count - 1

    barrier = pltpu.get_barrier_semaphore()
    for sector in (right, left):
        pl.semaphore_signal(barrier, inc=1, device_id=(ax, sector), device_id_type=MESH)

    @pl.when(has_low)
    def _():
        pl.semaphore_signal(barrier, inc=1, device_id=(ax - 1, az), device_id_type=MESH)

    @pl.when(has_high)
    def _():
        pl.semaphore_signal(barrier, inc=1, device_id=(ax + 1, az), device_id_type=MESH)

    load_cells = pltpu.make_async_copy(conserved, cells, load_sem.at[0])
    load_table = pltpu.make_async_copy(tables, table, load_sem.at[1])
    load_mode = pltpu.make_async_copy(modes, mode, load_sem.at[2])
    load_count = pltpu.make_async_copy(counts, count, load_sem.at[3])
    load_mode.start()
    load_count.start()
    load_cells.start()
    load_table.start()

    def tab(name):
        low, high = SPANS[name]
        return table[low:high]

    row = lax.broadcasted_iota(jnp.int32, (8, WIDTH), 0)
    lane = lax.broadcasted_iota(jnp.int32, (8, WIDTH), 1)
    lines_all = FIELDS * LINES
    for low, high in ((NEAR_ROWS, NEAR_PAD), (NEAR_PAD + NEAR_ROWS, 2 * NEAR_PAD), (2 * NEAR_PAD + FAR_ROWS, MESSAGE_ROWS)):
        message[low:high] = jnp.zeros((high - low, lines_all), jnp.float32)
    load_mode.wait()
    load_count.wait()
    mode_tiles = []
    for tile in range(ROWS // 8):
        value = jnp.zeros((8, WIDTH), jnp.int32)
        for j in range(8):
            value = jnp.where(row == j, mode[tile * 8 + j], value)
        mode_tiles.append(value)
    ring_modes = jnp.concatenate(mode_tiles, axis=0)
    inner_modes = jnp.zeros((8, WIDTH), jnp.int32)
    for j in range(4):
        inner_modes = jnp.where((row & 3) == j, mode[j], inner_modes)
    line_modes = jnp.zeros((8, WIDTH), jnp.int32)
    for j in range(ROWS):
        line_modes = jnp.where((lane & (ROWS - 1)) == j, mode[j], line_modes)
    edge_c, edge_s = waves(line_modes, az * WIDTH + row + jnp.where(row < 4, -4, WIDTH - 4))
    wave_c, wave_s = sector_waves(ring_modes, az)
    inner_c, inner_s = sector_waves(inner_modes, az)
    across_c, across_s = sector_waves(inner_modes, across)
    harmonic = lane & (MODE_MOST - 1)
    base_weight = jnp.where(harmonic == 0, 1.0 / NT, 2.0 / NT).astype(jnp.float32)
    ring_harmonic = lax.broadcasted_iota(jnp.int32, (ROWS, WIDTH), 1) & (MODE_MOST - 1)
    ring_base = jnp.where(ring_harmonic == 0, 1.0 / NT, 2.0 / NT).astype(jnp.float32)
    ring_weight = jnp.where(ring_harmonic < ring_modes, ring_base, 0.0)
    inner_weight = jnp.where(harmonic < inner_modes, base_weight, 0.0)
    ring_row = lax.broadcasted_iota(jnp.int32, (ROWS, WIDTH), 0)
    per_radius = TIME_STEP / (ring_row.astype(jnp.float32) + 0.5)

    load_cells.wait()
    for x in range(STATIONS):
        s0, s1, s2, s3, s4 = (cells[x, c] for c in range(FIELDS))
        inverse = 1.0 / s0
        a = s1 * inverse
        b = s2 * inverse
        d = s3 * inverse
        p = GAS_FACTOR * (s4 - 0.5 * (s1 * a + s2 * b + s3 * d))
        e = s4 + p
        lines = pl.ds(x * ROWS, ROWS)
        flux_f[x, 0], flux_f[x, 1], flux_f[x, 2], flux_f[x, 3], flux_f[x, 4] = s1, s1 * a + p, s2 * a, s3 * a, a * e
        for c, value in enumerate((s2, s1 * b, s2 * b + p, s3 * b, b * e)):
            flux_g[c, lines] = value
        swirl_two = s2 * d
        swirl_three = s3 * d + p
        for c, value in enumerate((s3, s1 * d, swirl_two, swirl_three, d * e)):
            flux_h[c, lines] = value * (per_radius * (NT / (2.0 * math.pi)))
        for c, value in enumerate((s0, s1, s2 + per_radius * swirl_three, s3 - per_radius * swirl_two, s4)):
            section[c, lines] = value
    for c in range(FIELDS):
        for i in range(STATIONS):
            own = from_low = to_high = to_low = None
            for s in range(STATIONS):
                value = flux_f[s, c]
                if s != i:
                    weight = TIME_STEP * STENCIL[abs(s - i) - 1] * (-1.0 if s > i else 1.0)
                    own = weight * value if own is None else own + weight * value
                if s >= i:
                    term = TIME_STEP * STENCIL[3 + i - s] * value
                    to_high = term if to_high is None else to_high + term
                if s <= i:
                    term = -TIME_STEP * STENCIL[3 + s - i] * value
                    to_low = term if to_low is None else to_low + term
            section[c, pl.ds(i * ROWS, ROWS)] += own
            axial_out[1, i, c] = to_high
            axial_out[0, i, c] = to_low
            edge_weight = TIME_STEP * sum(STENCIL[i:])
            pl.when(jnp.logical_not(has_low))(
                functools.partial(store, axial_in, (0, i, c), edge_weight * flux_f[0, c])
            )
            edge_weight = -TIME_STEP * sum(STENCIL[3 - i :])
            pl.when(jnp.logical_not(has_high))(
                functools.partial(store, axial_in, (1, i, c), edge_weight * flux_f[3, c])
            )

    load_table.wait()
    edges = matmul(tab("edge"), flux_h[...].reshape(FIELDS * LINES, WIDTH), ((1,), (1,)))
    pack(edge_out, edges[0:4], 0)
    pack(edge_out, edges[4:8], 1)
    edge_waves = jnp.concatenate(
        [edges * jnp.concatenate([edge_c] * FIELDS, axis=1), edges * jnp.concatenate([edge_s] * FIELDS, axis=1)], axis=0
    )
    from_edges[...] = matmul(tab("source_edge")[:, 0:16], edge_waves)
    mirror_table = tab("mirror")
    for c in range(FIELDS):
        value = MIRROR_SIGNS[c] * matmul(mirror_table, flux_g[c])
        mirror_out[pl.ds(16 * c, 16)] = value
        for half in range(2):
            lines = pl.ds(16 * c + 8 * half, 8)
            mirror_mod[lines, 0:WIDTH] = value[8 * half : 8 * half + 8] * across_c
            mirror_mod[lines, WIDTH : 2 * WIDTH] = value[8 * half : 8 * half + 8] * across_s
    mirror_mod[80:128] = jnp.zeros((48, 2 * WIDTH), jnp.float32)
    sources = jnp.concatenate([tab("source_a"), tab("source_b")], axis=1)
    extra = matmul(sources, mirror_mod[...], ((1,), (1,)))
    extra_out[0] = extra[0:NEAR_ROWS]
    extra_out[1] = extra[NEAR_PAD : NEAR_PAD + NEAR_ROWS]
    extra_own[...] = extra[2 * NEAR_PAD : 64]
    radial_table = tab("radial")
    swirl_table = tab("swirl")
    for c in range(FIELDS):
        section[c] += matmul(radial_table, flux_g[c]) + matmul(flux_h[c], swirl_table)

    def remote(source, target, slot, device):
        return pltpu.make_async_remote_copy(
            src_ref=source, dst_ref=target, send_sem=send_sem.at[slot], recv_sem=recv_sem.at[slot],
            device_id=device, device_id_type=MESH,
        )

    pl.semaphore_wait(barrier, 2 + has_low.astype(jnp.int32) + has_high.astype(jnp.int32))
    to_high = remote(axial_out.at[1], axial_in.at[0], 0, (ax + 1, az))
    to_low = remote(axial_out.at[0], axial_in.at[1], 1, (ax - 1, az))
    edge_left = remote(edge_out.at[0], edge_in.at[0], 2, (ax, left))
    edge_right = remote(edge_out.at[1], edge_in.at[1], 3, (ax, right))
    extra_left = remote(extra_out.at[0], extra_in.at[0], 5, (ax, left))
    extra_right = remote(extra_out.at[1], extra_in.at[1], 6, (ax, right))
    mirror_copy = remote(mirror_out, mirror_in, 4, (ax, across))
    far_copy = remote(far_out.at[0], far_in.at[0], 7, (ax, across))
    near_right = remote(near_out.at[0], near_in.at[0], 8, (ax, right))
    near_left = remote(near_out.at[1], near_in.at[1], 9, (ax, left))
    for sector in (right, left):
        pl.semaphore_signal(go_sem, inc=1, device_id=(ax, sector), device_id_type=MESH)
    pl.when(has_high)(to_high.start)
    pl.when(has_low)(to_low.start)
    edge_left.start()
    edge_right.start()
    extra_left.start()
    extra_right.start()
    pl.semaphore_wait(go_sem, 2)
    mirror_copy.start()

    pl.when(has_high)(to_low_wait(remote(axial_out.at[1], axial_in.at[1], 1, (ax + 1, az))))
    pl.when(has_low)(to_low_wait(remote(axial_out.at[0], axial_in.at[0], 0, (ax - 1, az))))
    for c in range(FIELDS):
        for x in range(STATIONS):
            lines = pl.ds(x * ROWS, ROWS)
            value = section[c, lines] + axial_in[0, x, c] + axial_in[1, x, c]
            section[c, lines] = value
            modulated[pl.ds(c * LINES + x * ROWS, ROWS), 0:WIDTH] = value * wave_c
            modulated[pl.ds(c * LINES + x * ROWS, ROWS), WIDTH : 2 * WIDTH] = value * wave_s
    messages = matmul(sources, modulated[...], ((1,), (1,))) + from_edges[0:MESSAGE_ROWS]
    pack(far_out, messages[2 * NEAR_PAD : 2 * NEAR_PAD + FAR_ROWS], 0)
    pack(near_out, messages[0:NEAR_ROWS], 0)
    pack(near_out, messages[NEAR_PAD : NEAR_PAD + NEAR_ROWS], 1)
    far_copy.start()
    mirror_copy.wait_send()
    near_right.start()
    near_left.start()

    edge_left.wait_recv()
    edge_right.wait_recv()
    edges = jnp.concatenate([unpack(edge_in, 4, 0), unpack(edge_in, 4, 1)], axis=0)
    place = tab("place")
    for c in range(FIELDS):
        section[c] += matmul(edges[:, c * LINES : (c + 1) * LINES], place, ((0,), (0,)))

    basis = tab("basis")
    for c in range(FIELDS):
        coefficients = matmul(section[c], basis)
        weighted = coefficients * jnp.concatenate([ring_weight] * STATIONS, axis=0)
        smoothed = matmul(weighted, basis, ((1,), (1,)))
        for x in range(STATIONS):
            modulated[pl.ds(c * LINES + x * ROWS, ROWS), 0:WIDTH] = smoothed[x * ROWS : (x + 1) * ROWS]

    part_row = lax.broadcasted_iota(jnp.int32, (64, 2 * WIDTH), 0)
    sign_left = jnp.where(az == 0, -1.0, 1.0)
    sign_right = jnp.where(az == SECTORS - 1, -1.0, 1.0)
    sign_across = jnp.where(az < 2, -1.0, 1.0)
    self_row = lax.broadcasted_iota(jnp.int32, (2 * NEAR_PAD, FIELDS * LINES), 0)
    from_edges[MESSAGE_ROWS : MESSAGE_ROWS + 2 * NEAR_PAD] = from_edges[
        MESSAGE_ROWS : MESSAGE_ROWS + 2 * NEAR_PAD
    ] * jnp.where(self_row < NEAR_PAD, sign_left, sign_right).astype(jnp.float32)
    signs = jnp.where(part_row < NEAR_PAD, sign_left, jnp.where(part_row < 2 * NEAR_PAD, sign_right, sign_across))
    targets = jnp.concatenate([tab("target_a"), tab("target_b")], axis=1) * signs.astype(jnp.float32)

    extra_left.wait_recv()
    extra_right.wait_recv()
    fill = jnp.zeros((NEAR_PAD - NEAR_ROWS, WIDTH), jnp.float32)
    extra = jnp.concatenate([extra_in[0], fill, extra_in[1], fill, extra_own[...]], axis=0)
    extra_field = matmul(extra, targets, ((0,), (0,)))
    mirror_copy.wait_recv()
    mirrored = mirror_in[...]
    weighted = matmul(mirrored, basis) * jnp.concatenate([inner_weight] * 10, axis=0)
    compact_smooth = matmul(weighted, basis, ((1,), (1,)))
    for c in range(FIELDS):
        for half in range(2):
            lines = pl.ds(16 * c + 8 * half, 8)
            low = 16 * c + 8 * half
            smooth = (
                compact_smooth[low : low + 8]
                + inner_s * extra_field[low : low + 8, 0:WIDTH]
                + inner_c * extra_field[low : low + 8, WIDTH : 2 * WIDTH]
            )
            limit = jnp.where(row < 4, count[2 * half], count[2 * half + 1])
            compact[lines] = jnp.where((row & 3) < limit, smooth, mirror_in[lines])

    far_copy.wait_recv()
    message[2 * NEAR_PAD : 2 * NEAR_PAD + FAR_ROWS] = unpack(far_in, FAR_ROWS, 0)
    near_right.wait_recv()
    message[0:NEAR_ROWS] = unpack(near_in, NEAR_ROWS, 0) + from_edges[MESSAGE_ROWS : MESSAGE_ROWS + NEAR_ROWS]
    near_left.wait_recv()
    own_left = MESSAGE_ROWS + NEAR_PAD
    message[NEAR_PAD : NEAR_PAD + NEAR_ROWS] = unpack(near_in, NEAR_ROWS, 1) + from_edges[own_left : own_left + NEAR_ROWS]
    for c in range(FIELDS):
        field = matmul(message[:, c * LINES : (c + 1) * LINES], targets, ((0,), (0,)))
        for x in range(STATIONS):
            low = x * ROWS
            smooth = (
                modulated[pl.ds(c * LINES + low, ROWS), 0:WIDTH]
                + wave_s * field[low : low + ROWS, 0:WIDTH]
                + wave_c * field[low : low + ROWS, WIDTH : 2 * WIDTH]
            )
            out[x, c] = jnp.where(ring_row < count[x], smooth, section[c, pl.ds(low, ROWS)])
            out[x, c, 0:4] += compact[pl.ds(16 * c + 4 * x, 4)]

    pl.when(has_high)(to_high.wait_send)
    pl.when(has_low)(to_low.wait_send)
    for copy in (edge_left, edge_right, extra_left, extra_right, far_copy, near_right, near_left):
        copy.wait_send()


def pack(ref, value, slot):
    rows = value.shape[0]
    for c in range(FIELDS):
        ref[slot, c * rows : (c + 1) * rows] = value[:, c * LINES : (c + 1) * LINES]


def unpack(ref, rows, slot):
    return jnp.concatenate([ref[slot, c * rows : (c + 1) * rows] for c in range(FIELDS)], axis=1)


def store(ref, index, value):
    ref[index] = value


def to_low_wait(copy):
    return copy.wait_recv


def per_device(conserved, cycle_modes, filtered_cycles):
    f32 = jnp.float32
    block = (STATIONS, FIELDS, ROWS, WIDTH)
    lines = FIELDS * LINES
    return pl.pallas_call(
        body,
        out_shape=jax.ShapeDtypeStruct(block, f32),
        in_specs=[
            pl.BlockSpec(memory_space=pltpu.HBM),
            pl.BlockSpec(memory_space=pltpu.HBM),
            pl.BlockSpec(memory_space=pltpu.HBM),
            pl.BlockSpec(memory_space=pltpu.HBM),
        ],
        out_specs=pl.BlockSpec(memory_space=pltpu.VMEM),
        scratch_shapes=[
            pltpu.VMEM(block, f32),
            pltpu.VMEM(TABLES.shape, f32),
            pltpu.SMEM((ROWS,), jnp.int32),
            pltpu.SMEM((STATIONS,), jnp.int32),
            pltpu.VMEM(block, f32),
            pltpu.VMEM((FIELDS, LINES, WIDTH), f32),
            pltpu.VMEM((FIELDS, LINES, WIDTH), f32),
            pltpu.VMEM((2,) + block, f32),
            pltpu.VMEM((2,) + block, f32),
            pltpu.VMEM((2, FIELDS * 4, LINES), f32),
            pltpu.VMEM((2, FIELDS * 4, LINES), f32),
            pltpu.VMEM((80, WIDTH), f32),
            pltpu.VMEM((80, WIDTH), f32),
            pltpu.VMEM((128, 2 * WIDTH), f32),
            pltpu.VMEM((2, NEAR_ROWS, WIDTH), f32),
            pltpu.VMEM((2, NEAR_ROWS, WIDTH), f32),
            pltpu.VMEM((16, WIDTH), f32),
            pltpu.VMEM((FIELDS, LINES, WIDTH), f32),
            pltpu.VMEM((lines, 2 * WIDTH), f32),
            pltpu.VMEM((2, FIELDS * NEAR_ROWS, LINES), f32),
            pltpu.VMEM((2, FIELDS * NEAR_ROWS, LINES), f32),
            pltpu.VMEM((1, FIELDS * FAR_ROWS, LINES), f32),
            pltpu.VMEM((1, FIELDS * FAR_ROWS, LINES), f32),
            pltpu.VMEM((MESSAGE_ROWS, lines), f32),
            pltpu.VMEM((2 * MESSAGE_ROWS, lines), f32),
            pltpu.VMEM((80, WIDTH), f32),
            pltpu.SemaphoreType.DMA((4,)),
            pltpu.SemaphoreType.DMA((10,)),
            pltpu.SemaphoreType.DMA((10,)),
            pltpu.SemaphoreType.REGULAR,
        ],
        compiler_params=pltpu.CompilerParams(
            collective_id=0, has_side_effects=True, vmem_limit_bytes=60 * 1024 * 1024
        ),
    )(conserved, jnp.asarray(TABLES), cycle_modes, filtered_cycles)


def solution(mesh):
    placed = (P("ax", None, None, "az"), P(), P("ax"))
    return jax.shard_map(
        per_device, mesh=mesh, in_specs=placed, out_specs=P("ax", None, None, "az"), check_vma=False
    )
```
